32 devices in a mesh: group: 4 (over y, x), dom: 8 (over z, core).
Axes of the slice: x: 2, y: 2, z: 4, core: 2. Of those that a mesh axis runs over, the one named last changes fastest.
Arguments:
- features: bfloat16 [16384, 128], P(('group', 'dom')), may hold values from -6 to 6
- adj_local: bfloat16 [16384, 512], P(('group', 'dom')), as said below
- adj_bound: bfloat16 [16384, 256], P(('group', 'dom')), as said below
- w_self: bfloat16 [128, 128], replicated, may hold values from -0.5 to 0.5
- w_neigh: bfloat16 [128, 128], replicated, may hold values from -0.5 to 0.5
- pub_rows: int32 [32, 64], P(('group', 'dom')), may hold values from 0 to 511, as said below
- recv_pos: int32 [32, 256], P(('group', 'dom')), may hold values from 0 to 63, as said below
- recv_count: int32 [32, 8], P(('group', 'dom')), may hold values from 0 to 32, as said below
- target_mask: int32 [16384], P(('group', 'dom')), may hold values from 0 to 1, as said below
- cotangent: bfloat16 [16384, 128], P(('group', 'dom')), may hold values from -6 to 6
Outputs:
- hidden_out: bfloat16 [16384, 128], P(('group', 'dom'))
- grad_features: bfloat16 [16384, 128], P(('group', 'dom'))
- grad_w_self: float32 [128, 128], replicated
- grad_w_neigh: float32 [128, 128], replicated
The draws below stay inside these ranges and needn't reach their ends.
Inputs may be any that keep to these rules, and one draw needn't show every extreme that they name: `pub_rows`: the 64 entries of a partition are distinct. `recv_pos`: for one partition and one peer the 32 positions are distinct. `recv_count`: A partition's count from itself is 0; in every group one partition receives 32 rows from every other partition of the group. `target_mask`: exactly 16 ones in every aligned block of 128 rows. `adj_local`: Nonnegative. `adj_bound`: Nonnegative.
All inputs are finite; a program needn't handle non-finite values.
Results may differ from the reference program's by a relative error of at most 0.0051.
Values may be sent and summed in bfloat16 or wider, within the bound.
No kernel may reach another device: no remote copies, remote signals or barrier semaphores. Data moves between devices by JAX's collectives and lax.ppermute only.
A program may use at most 64 MiB of HBM per device.

```python
import math
import jax
import jax.numpy as jnp
from jax import lax

D = 128
ROWS_DEV = 512
SLOT = 32
PUB = 64
NODES = 16384
TARGETS = 2048
N_GROUP = 4
N_DOM = 8
DEVICES = 32


def routing(key):
    key_order, key_count, key_full = jax.random.split(jax.random.fold_in(key, 101), 3)
    scores = jax.random.randint(key_order, (N_GROUP, N_DOM, N_DOM, PUB), 0, 1 << 20) * PUB + jnp.arange(PUB, dtype=jnp.int32)
    order = jnp.argsort(scores, axis=-1)[..., :SLOT].astype(jnp.int32)
    counts = jax.random.randint(key_count, (N_GROUP, N_DOM, N_DOM), 1, SLOT + 1)
    full_peer = jax.random.randint(key_full, (N_GROUP,), 0, N_DOM)
    peer_ids = jnp.arange(N_DOM, dtype=jnp.int32)
    counts = jnp.where(peer_ids[None, None, :] == full_peer[:, None, None], SLOT, counts)
    counts = jnp.where(peer_ids[:, None] == peer_ids[None, :], 0, counts)
    return (order, counts.astype(jnp.int32))


def draw_recv_pos(key, part):
    order, counts = routing(key)
    return jnp.transpose(order, (0, 2, 1, 3)).reshape(DEVICES, N_DOM * SLOT)


def draw_recv_count(key, part):
    order, counts = routing(key)
    return jnp.transpose(counts, (0, 2, 1)).reshape(DEVICES, N_DOM)


def draw_pub_rows(key, part):
    key = jax.random.fold_in(key, 3)
    scores = jax.random.randint(key, (DEVICES, ROWS_DEV), 0, 1 << 20) * ROWS_DEV + jnp.arange(ROWS_DEV, dtype=jnp.int32)
    return jnp.argsort(scores, axis=-1)[:, :PUB].astype(jnp.int32)


def draw_target_mask(key, part):
    key = jax.random.fold_in(key, 5)
    scores = jax.random.randint(key, (NODES // 128, 128), 0, 1 << 20) * 128 + jnp.arange(128, dtype=jnp.int32)
    ranks = jnp.argsort(jnp.argsort(scores, axis=-1), axis=-1)
    return (ranks < 16).astype(jnp.int32).reshape(NODES)


def edge_tile(key, shape, neighbours):
    key_edge, key_weight = jax.random.split(key)
    present = jax.random.uniform(key_edge, shape, jnp.float32) < neighbours / shape[1]
    weights = jnp.exp(jax.random.uniform(key_weight, shape, jnp.float32, -1.2, 1.2))
    return jnp.where(present, weights, 0.0).astype(jnp.bfloat16)


def draw_adj_local(key, part):
    key = jax.random.fold_in(key, 7)
    return edge_tile(key, (NODES, ROWS_DEV), 8.0)


def draw_adj_bound(key, part):
    key = jax.random.fold_in(key, 9)
    return edge_tile(key, (NODES, N_DOM * SLOT), 12.0)


def steps_of(rng, shape, pieces, smallest, largest):
    factor_of = 1.0
    for dim, blocks in pieces:
        heights = jax.random.uniform(jax.random.fold_in(jax.random.fold_in(rng, 6), dim), (blocks,), jnp.float32, smallest / len(pieces), largest / len(pieces))
        factor_of = factor_of * jnp.repeat(jnp.exp(heights), shape[dim] // blocks).reshape((-1,) + (1,) * (len(shape) - 1 - dim))
    return factor_of


def noise(key, extent, scale, limit, shards=(), kind=jnp.bfloat16):
    level = steps_of(key, extent, shards, -0.22, 0.18) if shards else 1.0
    result = jax.random.normal(key, extent, jnp.float32) * scale * level
    return jnp.minimum(jnp.maximum(result, -limit), limit).astype(kind)


def setup_inputs(seed: int = 0) -> dict:
    key_of = jax.random.split(jax.random.key(seed), 11)
    features = noise(key_of[0], (NODES, D), 1.0, 6.0, ((0, 32),))
    adj_local = draw_adj_local(jax.random.fold_in(key_of[10], 71), 0)
    adj_bound = draw_adj_bound(jax.random.fold_in(key_of[10], 71), 0)
    w_self = noise(key_of[3], (D, D), D ** -0.5, 0.5)
    w_neigh = noise(key_of[4], (D, D), D ** -0.5, 0.5)
    pub_rows = draw_pub_rows(jax.random.fold_in(key_of[10], 71), 0)
    recv_pos = draw_recv_pos(jax.random.fold_in(key_of[10], 71), 0)
    recv_count = draw_recv_count(jax.random.fold_in(key_of[10], 71), 0)
    target_mask = draw_target_mask(jax.random.fold_in(key_of[10], 71), 0)
    cotangent = noise(key_of[9], (NODES, D), 1.0, 6.0, ((0, 32),))
    return dict(features=features, adj_local=adj_local, adj_bound=adj_bound, w_self=w_self, w_neigh=w_neigh, pub_rows=pub_rows, recv_pos=recv_pos, recv_count=recv_count, target_mask=target_mask, cotangent=cotangent)


def silu_slope(preact):
    sigma = jax.nn.sigmoid(preact)
    return sigma * (1.0 + preact * (1.0 - sigma))

def reference(features, adj_local, adj_bound, w_self, w_neigh, pub_rows, recv_pos, recv_count, target_mask, cotangent):
    node_rows = features.reshape(DEVICES, ROWS_DEV, D)
    local_tiles = adj_local.reshape(DEVICES, ROWS_DEV, ROWS_DEV)
    bound_tiles = adj_bound.reshape(DEVICES, ROWS_DEV, N_DOM * SLOT)
    target_rows = target_mask.reshape(DEVICES, ROWS_DEV)
    upstream = cotangent.reshape(DEVICES, ROWS_DEV, D)
    slot_ids = jnp.arange(SLOT, dtype=jnp.int32)
    peer_ids = jnp.arange(N_DOM, dtype=jnp.int32)

    def device_step(totals, device):
        peer_sum, sum_self, sum_neigh = totals
        first_peer = device // N_DOM * N_DOM
        group_rows = lax.dynamic_slice_in_dim(node_rows, first_peer, N_DOM, 0)
        group_pub = lax.dynamic_slice_in_dim(pub_rows, first_peer, N_DOM, 0)
        positions = recv_pos[device].reshape(N_DOM, SLOT)
        source_rows = jnp.take_along_axis(group_pub, positions, axis=1)
        in_use = slot_ids[None, :] < recv_count[device][:, None]
        fetched = group_rows[peer_ids[:, None], source_rows]
        received = jnp.where(in_use[:, :, None], fetched, jnp.zeros_like(fetched)).reshape(N_DOM * SLOT, D)
        own_rows = node_rows[device]
        local_tile = local_tiles[device]
        bound_tile = jnp.where(in_use.reshape(1, -1), bound_tiles[device], jnp.zeros_like(bound_tiles[device]))
        weight_sum = lax.optimization_barrier(jnp.sum(local_tile, axis=1, dtype=jnp.float32)) + lax.optimization_barrier(jnp.sum(bound_tile, axis=1, dtype=jnp.float32))
        inverse_degree = (1.0 / (1.0 + weight_sum))[:, None]
        summed = jnp.dot(local_tile, own_rows, preferred_element_type=jnp.float32) + jnp.dot(bound_tile, received, preferred_element_type=jnp.float32)
        aggregate = (summed * inverse_degree).astype(jnp.bfloat16)
        preact = jnp.dot(own_rows, w_self, preferred_element_type=jnp.float32) + jnp.dot(aggregate, w_neigh, preferred_element_type=jnp.float32)
        hidden = jax.nn.silu(preact).astype(jnp.bfloat16)
        chosen = target_rows[device].astype(jnp.float32)[:, None]
        grad_pre = (upstream[device].astype(jnp.float32) * chosen * silu_slope(preact)).astype(jnp.bfloat16)
        grad_self = jnp.dot(own_rows.T, grad_pre, preferred_element_type=jnp.float32)
        grad_neigh = jnp.dot(aggregate.T, grad_pre, preferred_element_type=jnp.float32)
        grad_aggregate = (jnp.dot(grad_pre, w_neigh.T, preferred_element_type=jnp.float32) * inverse_degree).astype(jnp.bfloat16)
        grad_local = jnp.dot(grad_pre, w_self.T, preferred_element_type=jnp.float32) + jnp.dot(local_tile.T, grad_aggregate, preferred_element_type=jnp.float32)
        grad_received = jnp.dot(bound_tile.T, grad_aggregate, preferred_element_type=jnp.float32)
        global_rows = ((first_peer + peer_ids)[:, None] * ROWS_DEV + source_rows).reshape(-1).astype(jnp.int32)
        peer_sum = peer_sum.at[global_rows].add(grad_received)
        return ((peer_sum, sum_self + grad_self, sum_neigh + grad_neigh), (hidden, grad_local))
    start = (jnp.zeros((NODES, D), jnp.float32), jnp.zeros((D, D), jnp.float32), jnp.zeros((D, D), jnp.float32))
    totals, outputs = lax.scan(device_step, start, jnp.arange(DEVICES, dtype=jnp.int32))
    peer_sum, sum_self, sum_neigh = totals
    hiddens, grad_locals = outputs
    grad_features = (grad_locals.reshape(NODES, D) + peer_sum).astype(jnp.bfloat16)
    grad_scale = 1.0 / math.sqrt(TARGETS)
    return (hiddens.reshape(NODES, D), grad_features, sum_self * grad_scale, sum_neigh * grad_scale)
```

```python
import functools
import math

import jax
import jax.numpy as jnp
from jax import lax
from jax.experimental import pallas as pl
from jax.experimental.pallas import tpu as pltpu
from jax.sharding import PartitionSpec as P

BF = jnp.bfloat16
F32 = jnp.float32
VMEM = pl.BlockSpec(memory_space=pltpu.VMEM)
SMEM = pl.BlockSpec(memory_space=pltpu.SMEM)
PARAMS = pltpu.CompilerParams(vmem_limit_bytes=48 * 1024 * 1024)


def dot(a, b):
    return jnp.dot(a, b, preferred_element_type=F32)


def dot_t(a, b):
    return lax.dot_general(a, b, (((0,), (0,)), ((), ())), preferred_element_type=F32)


def dot_nt(a, b):
    return lax.dot_general(a, b, (((1,), (1,)), ((), ())), preferred_element_type=F32)


def one_hot(rows, targets):
    row = lax.broadcasted_iota(jnp.int32, (rows, targets.shape[1]), 0)
    return jnp.where(row == targets, 1.0, 0.0).astype(BF)


def call(body, outs, *args, smem=()):
    return pl.pallas_call(
        body,
        out_shape=[jax.ShapeDtypeStruct(shape, dtype) for shape, dtype in outs],
        in_specs=[SMEM if i in smem else VMEM for i in range(len(args))],
        out_specs=[VMEM] * len(outs),
        compiler_params=PARAMS,
    )(*args)


def xor_swap(x, axis, size, k):
    return lax.ppermute(x, axis, [(a, a ^ k) for a in range(size)])


def publish_body(pub_ref, features_ref, out_ref):
    out_ref[...] = dot_t(one_hot(features_ref.shape[0], pub_ref[...]), features_ref[...]).astype(BF)


def prepare_body(
    dom_size,
    pub_count,
    features_ref,
    local_ref,
    bound_ref,
    pos_ref,
    count_ref,
    w_self_ref,
    adj_ref,
    part_ref,
    inv_ref,
    self_ref,
):
    me = lax.axis_index("dom")
    slots = pos_ref.shape[1]
    slot_rows = slots // dom_size
    lane = lax.broadcasted_iota(jnp.int32, (1, slots), 1)
    peer = lane // slot_rows
    limit = jnp.zeros((1, slots), jnp.int32)
    for j in range(dom_size):
        limit = jnp.where(peer == j, count_ref[0, j], limit)
    in_use = lane % slot_rows < limit
    target = jnp.where(in_use, (peer ^ me) * pub_count + pos_ref[...], -1)
    columns = dom_size * pub_count
    chunk = math.gcd(columns, 512)
    features = features_ref[...]
    ones = jnp.ones(features.shape, BF)

    def move(c, total):
        start = pl.multiple_of(c * chunk, chunk)
        block = dot_nt(bound_ref[...], one_hot(chunk, target - start)).astype(BF)
        adj_ref[:, pl.ds(start, chunk)] = block
        return total + dot(block, jnp.ones((chunk, features.shape[1]), BF))

    sums = lax.fori_loop(0, columns // chunk, move, dot(local_ref[...], ones))
    inv_ref[...] = 1.0 / (1.0 + sums)
    part_ref[...] = dot(local_ref[...], features)
    self_ref[...] = dot(features, w_self_ref[...])


def layer_body(
    blocks,
    features_ref,
    local_ref,
    adj_ref,
    part_ref,
    inv_ref,
    self_ref,
    w_self_ref,
    w_neigh_ref,
    cot_ref,
    *refs,
):
    gathered = refs[:blocks]
    hidden_ref, local_grad_ref, keep_w_ref, send_w_ref, keep_g_ref, send_g_ref, rows_ref = refs[blocks:]
    pub_count = gathered[0].shape[0]
    for k in range(blocks):
        rows_ref[k * pub_count : (k + 1) * pub_count, :] = gathered[k][...]
    inv = inv_ref[...]
    aggregate = ((part_ref[...] + dot(adj_ref[...], rows_ref[...])) * inv).astype(BF)
    preact = self_ref[...] + dot(aggregate, w_neigh_ref[...])
    sigma = jax.nn.sigmoid(preact)
    hidden_ref[...] = (preact * sigma).astype(BF)
    slope = sigma * (1.0 + preact * (1.0 - sigma))
    grad_pre = (cot_ref[...].astype(F32) * slope).astype(BF)
    grad_agg = (dot_nt(grad_pre, w_neigh_ref[...]) * inv).astype(BF)
    grad_self = dot_t(features_ref[...], grad_pre)
    grad_neigh = dot_t(aggregate, grad_pre)
    first = lax.axis_index("dom") % 2 == 0
    keep_w_ref[...] = jnp.where(first, grad_self, grad_neigh)
    send_w_ref[...] = jnp.where(first, grad_neigh, grad_self)
    grad_rows = dot_t(adj_ref[...], grad_agg)
    for z in range(blocks // 2):
        here = slice(z * pub_count, (z + 1) * pub_count)
        even = slice(2 * z * pub_count, (2 * z + 1) * pub_count)
        odd = slice((2 * z + 1) * pub_count, (2 * z + 2) * pub_count)
        keep_g_ref[here, :] = grad_rows[even]
        send_g_ref[here, :] = grad_rows[odd].astype(BF)
    local_grad_ref[...] = dot_nt(grad_pre, w_self_ref[...]) + dot_t(local_ref[...], grad_agg)


def chip_body(group_size, pub_count, keep_w_ref, got_w_ref, keep_g_ref, got_g_ref, own_ref, far_ref, total_ref, *parts):
    grads = keep_g_ref[...] + got_g_ref[...].astype(F32)
    own_ref[...] = grads[:pub_count]
    far_ref[...] = grads[pub_count:].astype(BF)
    me = lax.axis_index("group")
    total_ref[...] = keep_w_ref[...] + got_w_ref[...]
    rows = parts[0].shape[0]
    for k in range(group_size):
        parts[k][...] = total_ref[pl.ds(pl.multiple_of((me ^ k) * rows, rows), rows), :]


def group_body(count, far_ref, *refs):
    parts, (total_ref, *messages) = refs[:count], refs[count:]
    total = parts[0][...]
    for part in parts[1:]:
        total = total + part[...]
    total_ref[...] = total
    high = total.astype(BF).astype(F32)
    halves = jnp.concatenate([high, total - high], axis=0).astype(BF)
    pub_count = far_ref.shape[0] // len(messages)
    for z, message in enumerate(messages):
        message[:pub_count, :] = far_ref[z * pub_count : (z + 1) * pub_count, :]
        message[pub_count:, :] = halves


def weights_body(scale, pub_count, total_ref, *refs):
    messages, (out_ref,) = refs[:-1], refs[-1:]
    total = total_ref[...]
    rows = total.shape[0]
    for message in messages:
        halves = message[pub_count:, :].astype(F32)
        total = total + halves[:rows] + halves[rows:]
    out_ref[...] = total * scale


def features_body(pub_ref, local_grad_ref, own_ref, *refs):
    messages, (out_ref,) = refs[:-1], refs[-1:]
    total = own_ref[...]
    for message in messages:
        total = total + message[: total.shape[0], :].astype(F32)
    place = one_hot(local_grad_ref.shape[0], pub_ref[...])
    high = total.astype(BF)
    low = (total - high.astype(F32)).astype(BF)
    out_ref[...] = (local_grad_ref[...] + dot(place, high) + dot(place, low)).astype(BF)


def place_body(count, *refs):
    mine, theirs, (self_ref, neigh_ref) = refs[:count], refs[count : 2 * count], refs[2 * count :]
    me = lax.axis_index("group")
    first = lax.axis_index("dom") % 2 == 0
    rows = mine[0].shape[0]
    for k in range(count):
        here = pl.ds(pl.multiple_of((me ^ k) * rows, rows), rows)
        a, b = mine[k][...], theirs[k][...]
        self_ref[here, :] = jnp.where(first, a, b)
        neigh_ref[here, :] = jnp.where(first, b, a)


def local(
    features,
    adj_local,
    adj_bound,
    w_self,
    w_neigh,
    pub_rows,
    recv_pos,
    recv_count,
    target_mask,
    cotangent,
):
    dom_size, group_size = lax.axis_size("dom"), lax.axis_size("group")
    z_size = dom_size // 2
    row_count, width = features.shape
    pub_count = pub_rows.shape[1]
    wide = (row_count, width)
    over_z = lambda x, z: xor_swap(x, "dom", dom_size, 2 * z)
    over_core = lambda x: xor_swap(x, "dom", dom_size, 1)
    over_group = lambda x, k: xor_swap(x, "group", group_size, k)

    (published,) = call(publish_body, [((pub_count, width), BF)], pub_rows, features)
    near = [published] + [over_z(published, z) for z in range(1, z_size)]
    far = [over_core(x) for x in near]
    gathered = [x for pair in zip(near, far) for x in pair]

    adj_rows, part, inverse, own_part = call(
        functools.partial(prepare_body, dom_size, pub_count),
        [((row_count, dom_size * pub_count), BF), (wide, F32), (wide, F32), (wide, F32)],
        features,
        adj_local,
        adj_bound,
        recv_pos,
        recv_count,
        w_self,
        smem=(4,),
    )
    chosen = jnp.where(target_mask[:, None] > 0, cotangent, jnp.zeros((), BF))
    slots_z = z_size * pub_count
    hidden, local_grad, keep_w, send_w, keep_g, send_g = pl.pallas_call(
        functools.partial(layer_body, dom_size),
        out_shape=[
            jax.ShapeDtypeStruct(s, d)
            for s, d in [
                (wide, BF),
                (wide, F32),
                ((width, width), F32),
                ((width, width), F32),
                ((slots_z, width), F32),
                ((slots_z, width), BF),
            ]
        ],
        in_specs=[VMEM] * (9 + dom_size),
        out_specs=[VMEM] * 6,
        scratch_shapes=[pltpu.VMEM((dom_size * pub_count, width), BF)],
        compiler_params=PARAMS,
    )(features, adj_local, adj_rows, part, inverse, own_part, w_self, w_neigh, chosen, *gathered)

    got_w, got_g = over_core(send_w), over_core(send_g)
    quarter = (width // group_size, width)
    own_g, far_g, _, *parts = call(
        functools.partial(chip_body, group_size, pub_count),
        [((pub_count, width), F32), ((slots_z - pub_count, width), BF), ((width, width), F32)]
        + [(quarter, F32)] * group_size,
        keep_w,
        got_w,
        keep_g,
        got_g,
    )
    got_parts = [parts[0]] + [over_group(parts[k], k) for k in range(1, group_size)]
    message = ((pub_count + 2 * quarter[0], width), BF)
    group_total, *messages = call(
        functools.partial(group_body, group_size), [(quarter, F32)] + [message] * (z_size - 1), far_g, *got_parts
    )
    got = [over_z(messages[z - 1], z) for z in range(1, z_size)]
    scale = 1.0 / math.sqrt(row_count * group_size * dom_size // 8)
    (total,) = call(functools.partial(weights_body, scale, pub_count), [(quarter, F32)], group_total, *got)
    mine = [total] + [over_group(total, k) for k in range(1, group_size)]
    theirs = [over_core(x) for x in mine]
    (grad_features,) = call(features_body, [(wide, BF)], pub_rows, local_grad, own_g, *got)
    grad_self, grad_neigh = call(
        functools.partial(place_body, group_size), [((width, width), F32)] * 2, *mine, *theirs
    )
    return hidden, grad_features, grad_self, grad_neigh


def solution(mesh):
    rows = P(("group", "dom"), None)
    in_specs = (rows, rows, rows, P(), P(), rows, rows, rows, P(("group", "dom")), rows)
    return jax.shard_map(
        local, mesh=mesh, in_specs=in_specs, out_specs=(rows, rows, P(), P()), check_vma=False
    )
```

```python
import functools
import math

import jax
import jax.numpy as jnp
from jax import lax
from jax.experimental import pallas as pl
from jax.experimental.pallas import tpu as pltpu
from jax.sharding import PartitionSpec as P

BF = jnp.bfloat16
F32 = jnp.float32
VMEM = pl.BlockSpec(memory_space=pltpu.VMEM)
HBM = pl.BlockSpec(memory_space=pltpu.HBM)
PARAMS = pltpu.CompilerParams(vmem_limit_bytes=48 * 1024 * 1024)


def dot(a, b):
    return jnp.dot(a, b, preferred_element_type=F32)


def dot_t(a, b):
    return lax.dot_general(a, b, (((0,), (0,)), ((), ())), preferred_element_type=F32)


def dot_nt(a, b):
    return lax.dot_general(a, b, (((1,), (1,)), ((), ())), preferred_element_type=F32)


def one_hot(rows, targets):
    row = lax.broadcasted_iota(jnp.int32, (rows, targets.shape[1]), 0)
    return jnp.where(row == targets, 1.0, 0.0).astype(BF)


def in_hbm(x):
    return pltpu.with_memory_space_constraint(x, pltpu.HBM)


def call(body, outs, *args):
    return pl.pallas_call(
        body,
        out_shape=[jax.ShapeDtypeStruct(shape, dtype) for shape, dtype in outs],
        in_specs=[VMEM] * len(args),
        out_specs=[VMEM] * len(outs),
        compiler_params=PARAMS,
    )(*args)


def odd_core():
    return lax.axis_index("dom") % 2 == 1


def tree_sum(parts):
    while len(parts) > 1:
        parts = [a + b for a, b in zip(parts[::2], parts[1::2])]
    return parts[0]


def load(pairs, sems):
    copies = [pltpu.make_async_copy(a, b, sems.at[i]) for i, (a, b) in enumerate(pairs)]
    for copy in copies:
        copy.start()
    return copies


def publish_body(count, *refs):
    sources, (out_ref, *targets), sems = refs[:count], refs[count:-1], refs[-1]
    pub, rows, *rest = load(list(zip(sources, targets)), sems)
    pub_ref, features_ref = targets[:2]
    pub_count = pub_ref.shape[1]
    square = (pub_count, pub_count)
    pub.wait()
    diagonal = lax.broadcasted_iota(jnp.int32, square, 0) == lax.broadcasted_iota(jnp.int32, square, 1)
    column = jnp.sum(jnp.where(diagonal, pub_ref[...].astype(F32), 0.0), axis=1, keepdims=True)
    row = lax.broadcasted_iota(jnp.int32, (pub_count, features_ref.shape[0]), 1)
    pick = jnp.where(row == column.astype(jnp.int32), 1.0, 0.0).astype(BF)
    rows.wait()
    out_ref[...] = dot(pick, features_ref[...]).astype(BF)
    for copy in rest:
        copy.wait()


def pair_body(own_ref, other_ref, out_ref):
    rows = own_ref.shape[0]
    odd = odd_core()
    own, other = own_ref[...], other_ref[...]
    out_ref[:rows, :] = jnp.where(odd, other, own)
    out_ref[rows:, :] = jnp.where(odd, own, other)


def prepare_body(
    dom_size,
    pub_ref,
    features_ref,
    local_ref,
    bound_ref,
    w_self_ref,
    pos_ref,
    count_ref,
    mask_ref,
    cot_ref,
    place_ref,
    adj_ref,
    flip_ref,
    part_ref,
    inv_ref,
    self_ref,
    chosen_ref,
):
    pub_count = pub_ref.shape[1]
    place_ref[...] = one_hot(features_ref.shape[0], pub_ref[...])
    features = features_ref[...]
    self_ref[...] = dot(features, w_self_ref[...])
    me = lax.axis_index("dom")
    chip = me - me % 2
    slots = pos_ref.shape[1]
    slot_rows = slots // dom_size
    lane = lax.broadcasted_iota(jnp.int32, (1, slots), 1)
    peer = lane // slot_rows
    limit = jnp.zeros((1, slots), jnp.int32)
    for j in range(dom_size):
        limit = jnp.where(peer == j, count_ref[0:1, j : j + 1], limit)
    in_use = lane % slot_rows < limit
    target = jnp.where(in_use, (peer ^ chip) * pub_count + pos_ref[...], -1)
    columns = dom_size * pub_count
    chunk = math.gcd(columns, 512)

    def move(c, total):
        here = pl.ds(pl.multiple_of(c * chunk, chunk), chunk)
        moves = one_hot(chunk, target - c * chunk)
        block = dot_nt(bound_ref[...], moves).astype(BF)
        adj_ref[:, here] = block
        flip_ref[here, :] = dot_nt(moves, bound_ref[...]).astype(BF)
        return total + dot(block, jnp.ones((chunk, features.shape[1]), BF))

    sums = lax.fori_loop(0, columns // chunk, move, jnp.zeros(features.shape, F32))
    first = lax.broadcasted_iota(jnp.int32, (8, mask_ref.shape[1]), 0) == 0
    mask = jnp.where(first & (mask_ref[...] > 0), 1.0, 0.0).astype(BF)
    chosen = dot_t(mask, jnp.ones((8, features.shape[1]), BF))
    chosen_ref[...] = (cot_ref[...].astype(F32) * chosen).astype(BF)
    part_ref[...] = dot(local_ref[...], features)
    inv_ref[...] = 1.0 / (1.0 + sums + dot(local_ref[...], jnp.ones(features.shape, BF)))


def layer_body(
    z_size,
    features_ref,
    adj_ref,
    flip_ref,
    part_ref,
    inv_ref,
    self_ref,
    w_neigh_ref,
    cot_ref,
    *refs,
):
    pairs, refs = refs[:z_size], refs[z_size:]
    hidden_ref, pre_ref, agg_ref, weights_ref, grads_ref, rounded_ref, rows_ref = refs
    count = pairs[0].shape[0]
    for z, pair in enumerate(pairs):
        rows_ref[z * count : (z + 1) * count, :] = pair[...]
    inv = inv_ref[...]
    aggregate = ((part_ref[...] + dot(adj_ref[...], rows_ref[...])) * inv).astype(BF)
    preact = self_ref[...] + dot(aggregate, w_neigh_ref[...])
    sigma = jax.nn.sigmoid(preact)
    hidden_ref[...] = (preact * sigma).astype(BF)
    slope = sigma * (1.0 + preact * (1.0 - sigma))
    grad_pre = (cot_ref[...].astype(F32) * slope).astype(BF)
    grad_agg = (dot_nt(grad_pre, w_neigh_ref[...]) * inv).astype(BF)
    pre_ref[...] = grad_pre
    agg_ref[...] = grad_agg
    width = features_ref.shape[1]
    weights_ref[:width, :] = dot_t(features_ref[...], grad_pre)
    weights_ref[width:, :] = dot_t(aggregate, grad_pre)
    grads = dot(flip_ref[...], grad_agg)
    grads_ref[...] = grads
    rounded_ref[...] = grads.astype(BF)


def local_body(local_ref, w_self_ref, pre_ref, agg_ref, out_ref):
    out_ref[...] = dot_nt(pre_ref[...], w_self_ref[...]) + dot_t(local_ref[...], agg_ref[...])


def chip_body(weights_ref, got_w_ref, grads_ref, got_g_ref, own_ref, total_ref, *messages):
    grads = grads_ref[...] + got_g_ref[...].astype(F32)
    rows = own_ref.shape[0]
    own_ref[...] = grads[:rows]
    total = (weights_ref[...] + got_w_ref[...]).astype(BF)
    total_ref[...] = total
    for z, message in zip(range(len(messages), 0, -1), messages):
        message[:rows, :] = grads[z * rows : (z + 1) * rows].astype(BF)
        message[rows:, :] = total


def column_body(scale, total_ref, own_ref, *refs):
    messages, (out_ref, even_ref, odd_ref) = refs[:-3], refs[-3:]
    rows = own_ref.shape[0]
    parts = [total_ref[...]] + [message[rows:, :] for message in messages]
    out_ref[...] = (tree_sum([part.astype(F32) for part in parts]) * scale).astype(BF)
    grads = own_ref[...]
    for message in messages:
        grads = grads + message[:rows, :].astype(F32)
    even_ref[...] = grads[: rows // 2]
    odd_ref[...] = grads[rows // 2 :]


def features_body(hidden_ref, place_ref, local_grad_ref, odd_ref, even_ref, hidden_out, out_ref):
    hidden_out[...] = hidden_ref[...]
    total = jnp.where(odd_core(), odd_ref[...], even_ref[...])
    place = place_ref[...]
    high = total.astype(BF)
    low = (total - high.astype(F32)).astype(BF)
    out_ref[...] = (local_grad_ref[...] + dot(place, high) + dot(place, low)).astype(BF)


def sum_body(*refs):
    refs[-1][...] = tree_sum([part[...].astype(F32) for part in refs[:-1]])


def order_body(mine_ref, other_ref, self_ref, neigh_ref):
    total = jnp.where(odd_core(), mine_ref[...], other_ref[...])
    width = self_ref.shape[0]
    self_ref[...] = total[:width]
    neigh_ref[...] = total[width:]


def local(
    features,
    adj_local,
    adj_bound,
    w_self,
    w_neigh,
    pub_rows,
    recv_pos,
    recv_count,
    target_mask,
    cotangent,
):
    dom_size, group_size = lax.axis_size("dom"), lax.axis_size("group")
    z_size = dom_size // 2
    row_count, width = features.shape
    pub_count = pub_rows.shape[1]
    wide = (row_count, width)
    devices = range(group_size * dom_size)

    def exchange(x, odd_step, even_step):
        return lax.ppermute(x, ("group", "dom"), [(a, a ^ (odd_step if a % 2 else even_step)) for a in devices])

    def over_core(x):
        return exchange(x, 1, 1)

    fetched = (
        pub_rows,
        features,
        adj_local,
        adj_bound,
        w_self,
        w_neigh,
        recv_pos,
        recv_count,
        target_mask.reshape(1, row_count),
        cotangent,
    )
    published, *fetched = pl.pallas_call(
        functools.partial(publish_body, len(fetched)),
        out_shape=[jax.ShapeDtypeStruct((pub_count, width), BF)]
        + [jax.ShapeDtypeStruct(x.shape, x.dtype) for x in fetched],
        in_specs=[HBM] * len(fetched),
        out_specs=[VMEM] * (1 + len(fetched)),
        scratch_shapes=[pltpu.SemaphoreType.DMA((len(fetched),))],
        compiler_params=PARAMS,
    )(*(in_hbm(x) for x in fetched))
    pub_rows, features, adj_local, adj_bound, w_self, w_neigh, recv_pos, recv_count, mask, cotangent = fetched
    (pair,) = call(pair_body, [((2 * pub_count, width), BF)], published, over_core(published))
    pairs = [pair] + [exchange(pair, 2 * z, 2 * z) for z in range(1, z_size)]

    columns = dom_size * pub_count
    place, adj_rows, adj_flip, part, inverse, own_part, chosen = call(
        functools.partial(prepare_body, dom_size),
        [
            ((row_count, pub_count), BF),
            ((row_count, columns), BF),
            ((columns, row_count), BF),
            (wide, F32),
            (wide, F32),
            (wide, F32),
            (wide, BF),
        ],
        pub_rows,
        features,
        adj_local,
        adj_bound,
        w_self,
        recv_pos,
        recv_count,
        mask,
        cotangent,
    )
    square, both = (width, width), (2 * width, width)
    hidden, grad_pre, grad_agg, weights, grads, rounded = pl.pallas_call(
        functools.partial(layer_body, z_size),
        out_shape=[
            jax.ShapeDtypeStruct(s, d)
            for s, d in [
                (wide, BF),
                (wide, BF),
                (wide, BF),
                (both, F32),
                ((columns, width), F32),
                ((columns, width), BF),
            ]
        ],
        in_specs=[VMEM] * (8 + z_size),
        out_specs=[VMEM] * 6,
        scratch_shapes=[pltpu.VMEM((columns, width), BF)],
        compiler_params=PARAMS,
    )(features, adj_rows, adj_flip, part, inverse, own_part, w_neigh, chosen, *pairs)
    (local_grad,) = call(local_body, [(wide, F32)], adj_local, w_self, grad_pre, grad_agg)

    message = ((2 * pub_count + 2 * width, width), BF)
    own_g, chip_w, *messages = call(
        chip_body,
        [((2 * pub_count, width), F32), (both, BF)] + [message] * (z_size - 1),
        weights,
        over_core(weights),
        grads,
        over_core(rounded),
    )
    far = range(z_size - 1, 0, -1)
    arrived = [exchange(x, 2 * z, dom_size) for z, x in zip(far, messages)][::-1]
    scale = 1.0 / math.sqrt(row_count * group_size * dom_size // 8)
    column_w, even_g, odd_g = call(
        functools.partial(column_body, scale),
        [(both, BF)] + [((pub_count, width), F32)] * 2,
        chip_w,
        own_g,
        *arrived,
    )
    others = [exchange(column_w, dom_size * k, 2) for k in range(1, group_size)]
    *others, even_g, local_grad = lax.optimization_barrier((*others, over_core(even_g), local_grad))
    hidden, grad_features = call(features_body, [(wide, BF)] * 2, hidden, place, local_grad, odd_g, even_g)
    (mine,) = call(sum_body, [(both, F32)], column_w, *others)
    grad_self, grad_neigh = call(order_body, [(square, F32)] * 2, mine, over_core(mine))
    return hidden, grad_features, grad_self, grad_neigh


def solution(mesh):
    rows = P(("group", "dom"), None)
    in_specs = (rows, rows, rows, P(), P(), rows, rows, rows, P(("group", "dom")), rows)
    return jax.shard_map(
        local, mesh=mesh, in_specs=in_specs, out_specs=(rows, rows, P(), P()), check_vma=False
    )
```

```python
import functools
import math

import jax
import jax.numpy as jnp
from jax import lax
from jax.experimental import pallas as pl
from jax.experimental.pallas import tpu as pltpu
from jax.sharding import PartitionSpec as P

BF = jnp.bfloat16
F32 = jnp.float32
VMEM = pl.BlockSpec(memory_space=pltpu.VMEM)
HBM = pl.BlockSpec(memory_space=pltpu.HBM)
PARAMS = pltpu.CompilerParams(vmem_limit_bytes=48 * 1024 * 1024)


def dot(a, b):
    return jnp.dot(a, b, preferred_element_type=F32)


def dot_t(a, b):
    return lax.dot_general(a, b, (((0,), (0,)), ((), ())), preferred_element_type=F32)


def dot_nt(a, b):
    return lax.dot_general(a, b, (((1,), (1,)), ((), ())), preferred_element_type=F32)


def one_hot(rows, targets):
    row = lax.broadcasted_iota(jnp.int32, (rows, targets.shape[1]), 0)
    return jnp.where(row == targets, 1.0, 0.0).astype(BF)


def in_hbm(x):
    return pltpu.with_memory_space_constraint(x, pltpu.HBM)


def call(body, outs, *args):
    return pl.pallas_call(
        body,
        out_shape=[jax.ShapeDtypeStruct(shape, dtype) for shape, dtype in outs],
        in_specs=[VMEM] * len(args),
        out_specs=[VMEM] * len(outs),
        compiler_params=PARAMS,
    )(*args)


def odd_core():
    return lax.axis_index("dom") % 2 == 1


def tree_sum(parts):
    while len(parts) > 1:
        parts = [a + b for a, b in zip(parts[::2], parts[1::2])]
    return parts[0]


def load(pairs, sems):
    copies = [pltpu.make_async_copy(a, b, sems.at[i]) for i, (a, b) in enumerate(pairs)]
    for copy in copies:
        copy.start()
    return copies


def publish_body(pub_hbm, features_hbm, out_ref, pub_ref, features_ref, sems):
    pub, rows = load([(pub_hbm, pub_ref), (features_hbm, features_ref)], sems)
    pub_count = pub_ref.shape[1]
    square = (pub_count, pub_count)
    pub.wait()
    diagonal = lax.broadcasted_iota(jnp.int32, square, 0) == lax.broadcasted_iota(jnp.int32, square, 1)
    column = jnp.sum(jnp.where(diagonal, pub_ref[...].astype(F32), 0.0), axis=1, keepdims=True)
    row = lax.broadcasted_iota(jnp.int32, (pub_count, features_ref.shape[0]), 1)
    pick = jnp.where(row == column.astype(jnp.int32), 1.0, 0.0).astype(BF)
    rows.wait()
    out_ref[...] = dot(pick, features_ref[...]).astype(BF)


def pair_body(own_ref, other_ref, out_ref):
    rows = own_ref.shape[0]
    odd = odd_core()
    own, other = own_ref[...], other_ref[...]
    out_ref[:rows, :] = jnp.where(odd, other, own)
    out_ref[rows:, :] = jnp.where(odd, own, other)


def prepare_body(
    dom_size,
    pub_ref,
    features_ref,
    pos_hbm,
    count_hbm,
    mask_hbm,
    bound_hbm,
    cot_hbm,
    w_self_hbm,
    w_neigh_hbm,
    local_hbm,
    place_ref,
    adj_ref,
    flip_ref,
    part_ref,
    inv_ref,
    self_ref,
    chosen_ref,
    w_self_ref,
    w_neigh_ref,
    local_ref,
    pos_ref,
    count_ref,
    mask_ref,
    bound_ref,
    cot_ref,
    sems,
):
    copies = load(
        [
            (pos_hbm, pos_ref),
            (count_hbm, count_ref),
            (mask_hbm, mask_ref),
            (bound_hbm, bound_ref),
            (w_self_hbm, w_self_ref),
            (cot_hbm, cot_ref),
            (local_hbm, local_ref),
            (w_neigh_hbm, w_neigh_ref),
        ],
        sems,
    )
    pub_count = pub_ref.shape[1]
    place_ref[...] = one_hot(features_ref.shape[0], pub_ref[...])
    for copy in copies:
        copy.wait()
    features = features_ref[...]
    self_ref[...] = dot(features, w_self_ref[...])
    me = lax.axis_index("dom")
    chip = me - me % 2
    slots = pos_ref.shape[1]
    slot_rows = slots // dom_size
    lane = lax.broadcasted_iota(jnp.int32, (1, slots), 1)
    peer = lane // slot_rows
    limit = jnp.zeros((1, slots), jnp.int32)
    for j in range(dom_size):
        limit = jnp.where(peer == j, count_ref[0:1, j : j + 1], limit)
    in_use = lane % slot_rows < limit
    target = jnp.where(in_use, (peer ^ chip) * pub_count + pos_ref[...], -1)
    columns = dom_size * pub_count
    chunk = math.gcd(columns, 512)

    def move(c, total):
        here = pl.ds(pl.multiple_of(c * chunk, chunk), chunk)
        moves = one_hot(chunk, target - c * chunk)
        block = dot_nt(bound_ref[...], moves).astype(BF)
        adj_ref[:, here] = block
        flip_ref[here, :] = dot_nt(moves, bound_ref[...]).astype(BF)
        return total + dot(block, jnp.ones((chunk, features.shape[1]), BF))

    sums = lax.fori_loop(0, columns // chunk, move, jnp.zeros(features.shape, F32))
    first = lax.broadcasted_iota(jnp.int32, (8, mask_ref.shape[1]), 0) == 0
    mask = jnp.where(first & (mask_ref[...] > 0), 1.0, 0.0).astype(BF)
    chosen = dot_t(mask, jnp.ones((8, features.shape[1]), BF))
    chosen_ref[...] = (cot_ref[...].astype(F32) * chosen).astype(BF)
    part_ref[...] = dot(local_ref[...], features)
    inv_ref[...] = 1.0 / (1.0 + sums + dot(local_ref[...], jnp.ones(features.shape, BF)))


def layer_body(
    z_size,
    features_ref,
    adj_ref,
    flip_ref,
    part_ref,
    inv_ref,
    self_ref,
    w_neigh_ref,
    cot_ref,
    *refs,
):
    pairs, refs = refs[:z_size], refs[z_size:]
    hidden_ref, pre_ref, agg_ref, weights_ref, grads_ref, rounded_ref, rows_ref = refs
    count = pairs[0].shape[0]
    for z, pair in enumerate(pairs):
        rows_ref[z * count : (z + 1) * count, :] = pair[...]
    inv = inv_ref[...]
    aggregate = ((part_ref[...] + dot(adj_ref[...], rows_ref[...])) * inv).astype(BF)
    preact = self_ref[...] + dot(aggregate, w_neigh_ref[...])
    sigma = jax.nn.sigmoid(preact)
    hidden_ref[...] = (preact * sigma).astype(BF)
    slope = sigma * (1.0 + preact * (1.0 - sigma))
    grad_pre = (cot_ref[...].astype(F32) * slope).astype(BF)
    grad_agg = (dot_nt(grad_pre, w_neigh_ref[...]) * inv).astype(BF)
    pre_ref[...] = grad_pre
    agg_ref[...] = grad_agg
    width = features_ref.shape[1]
    weights_ref[:width, :] = dot_t(features_ref[...], grad_pre)
    weights_ref[width:, :] = dot_t(aggregate, grad_pre)
    grads = dot(flip_ref[...], grad_agg)
    grads_ref[...] = grads
    rounded_ref[...] = grads.astype(BF)


def local_body(local_ref, w_self_ref, pre_ref, agg_ref, out_ref):
    out_ref[...] = dot_nt(pre_ref[...], w_self_ref[...]) + dot_t(local_ref[...], agg_ref[...])


def chip_body(weights_ref, got_w_ref, grads_ref, got_g_ref, own_ref, total_ref, *messages):
    grads = grads_ref[...] + got_g_ref[...].astype(F32)
    rows = own_ref.shape[0]
    own_ref[...] = grads[:rows]
    total = (weights_ref[...] + got_w_ref[...]).astype(BF)
    total_ref[...] = total
    for z, message in zip(range(len(messages), 0, -1), messages):
        message[:rows, :] = grads[z * rows : (z + 1) * rows].astype(BF)
        message[rows:, :] = total


def column_body(scale, total_ref, own_ref, *refs):
    messages, (out_ref, even_ref, odd_ref) = refs[:-3], refs[-3:]
    rows = own_ref.shape[0]
    parts = [total_ref[...]] + [message[rows:, :] for message in messages]
    out_ref[...] = (tree_sum([part.astype(F32) for part in parts]) * scale).astype(BF)
    grads = own_ref[...]
    for message in messages:
        grads = grads + message[:rows, :].astype(F32)
    even_ref[...] = grads[: rows // 2]
    odd_ref[...] = grads[rows // 2 :]


def features_body(hidden_ref, place_ref, local_grad_ref, odd_ref, even_ref, hidden_out, out_ref):
    hidden_out[...] = hidden_ref[...]
    total = jnp.where(odd_core(), odd_ref[...], even_ref[...])
    place = place_ref[...]
    high = total.astype(BF)
    low = (total - high.astype(F32)).astype(BF)
    out_ref[...] = (local_grad_ref[...] + dot(place, high) + dot(place, low)).astype(BF)


def sum_body(*refs):
    refs[-1][...] = tree_sum([part[...].astype(F32) for part in refs[:-1]])


def order_body(mine_ref, other_ref, self_ref, neigh_ref):
    total = jnp.where(odd_core(), mine_ref[...], other_ref[...])
    width = self_ref.shape[0]
    self_ref[...] = total[:width]
    neigh_ref[...] = total[width:]


def local(
    features,
    adj_local,
    adj_bound,
    w_self,
    w_neigh,
    pub_rows,
    recv_pos,
    recv_count,
    target_mask,
    cotangent,
):
    dom_size, group_size = lax.axis_size("dom"), lax.axis_size("group")
    z_size = dom_size // 2
    row_count, width = features.shape
    pub_count = pub_rows.shape[1]
    wide = (row_count, width)
    devices = range(group_size * dom_size)

    def exchange(x, odd_step, even_step):
        return lax.ppermute(x, ("group", "dom"), [(a, a ^ (odd_step if a % 2 else even_step)) for a in devices])

    def over_core(x):
        return exchange(x, 1, 1)

    published, pub_rows, features = pl.pallas_call(
        publish_body,
        out_shape=[
            jax.ShapeDtypeStruct((pub_count, width), BF),
            jax.ShapeDtypeStruct(pub_rows.shape, jnp.int32),
            jax.ShapeDtypeStruct(wide, BF),
        ],
        in_specs=[HBM] * 2,
        out_specs=[VMEM] * 3,
        scratch_shapes=[pltpu.SemaphoreType.DMA((2,))],
        compiler_params=PARAMS,
    )(in_hbm(pub_rows), in_hbm(features))
    (pair,) = call(pair_body, [((2 * pub_count, width), BF)], published, over_core(published))
    pairs = [pair] + [exchange(pair, 2 * z, 2 * z) for z in range(1, z_size)]

    columns = dom_size * pub_count
    mask = target_mask.reshape(1, row_count)
    place, adj_rows, adj_flip, part, inverse, own_part, chosen, w_self, w_neigh, adj_local = pl.pallas_call(
        functools.partial(prepare_body, dom_size),
        out_shape=[
            jax.ShapeDtypeStruct(s, d)
            for s, d in [
                ((row_count, pub_count), BF),
                ((row_count, columns), BF),
                ((columns, row_count), BF),
                (wide, F32),
                (wide, F32),
                (wide, F32),
                (wide, BF),
                (w_self.shape, BF),
                (w_neigh.shape, BF),
                (adj_local.shape, BF),
            ]
        ],
        in_specs=[VMEM] * 2 + [HBM] * 8,
        out_specs=[VMEM] * 10,
        scratch_shapes=[pltpu.VMEM(x.shape, x.dtype) for x in (recv_pos, recv_count, mask, adj_bound, cotangent)]
        + [pltpu.SemaphoreType.DMA((8,))],
        compiler_params=PARAMS,
    )(
        pub_rows,
        features,
        *(in_hbm(x) for x in (recv_pos, recv_count, mask, adj_bound, cotangent, w_self, w_neigh, adj_local)),
    )
    square, both = (width, width), (2 * width, width)
    hidden, grad_pre, grad_agg, weights, grads, rounded = pl.pallas_call(
        functools.partial(layer_body, z_size),
        out_shape=[
            jax.ShapeDtypeStruct(s, d)
            for s, d in [
                (wide, BF),
                (wide, BF),
                (wide, BF),
                (both, F32),
                ((columns, width), F32),
                ((columns, width), BF),
            ]
        ],
        in_specs=[VMEM] * (8 + z_size),
        out_specs=[VMEM] * 6,
        scratch_shapes=[pltpu.VMEM((columns, width), BF)],
        compiler_params=PARAMS,
    )(features, adj_rows, adj_flip, part, inverse, own_part, w_neigh, chosen, *pairs)
    (local_grad,) = call(local_body, [(wide, F32)], adj_local, w_self, grad_pre, grad_agg)

    message = ((2 * pub_count + 2 * width, width), BF)
    own_g, chip_w, *messages = call(
        chip_body,
        [((2 * pub_count, width), F32), (both, BF)] + [message] * (z_size - 1),
        weights,
        over_core(weights),
        grads,
        over_core(rounded),
    )
    far = range(z_size - 1, 0, -1)
    arrived = [exchange(x, 2 * z, dom_size) for z, x in zip(far, messages)][::-1]
    scale = 1.0 / math.sqrt(row_count * group_size * dom_size // 8)
    column_w, even_g, odd_g = call(
        functools.partial(column_body, scale),
        [(both, BF)] + [((pub_count, width), F32)] * 2,
        chip_w,
        own_g,
        *arrived,
    )
    others = [exchange(column_w, dom_size * k, 2) for k in range(1, group_size)]
    *others, even_g, local_grad = lax.optimization_barrier((*others, over_core(even_g), local_grad))
    hidden, grad_features = call(features_body, [(wide, BF)] * 2, hidden, place, local_grad, odd_g, even_g)
    (mine,) = call(sum_body, [(both, F32)], column_w, *others)
    grad_self, grad_neigh = call(order_body, [(square, F32)] * 2, mine, over_core(mine))
    return hidden, grad_features, grad_self, grad_neigh


def solution(mesh):
    rows = P(("group", "dom"), None)
    in_specs = (rows, rows, rows, P(), P(), rows, rows, rows, P(("group", "dom")), rows)
    return jax.shard_map(
        local, mesh=mesh, in_specs=in_specs, out_specs=(rows, rows, P(), P()), check_vma=False
    )
```

```python
import functools
import math

import jax
import jax.numpy as jnp
from jax import lax
from jax.experimental import pallas as pl
from jax.experimental.pallas import tpu as pltpu
from jax.sharding import PartitionSpec as P

BF = jnp.bfloat16
F32 = jnp.float32
BLOCK, HITS = 128, 16
VMEM = pl.BlockSpec(memory_space=pltpu.VMEM)
HBM = pl.BlockSpec(memory_space=pltpu.HBM)
PARAMS = pltpu.CompilerParams(vmem_limit_bytes=48 * 1024 * 1024)


def dot(a, b):
    return jnp.dot(a, b, preferred_element_type=F32)


def dot_t(a, b):
    return lax.dot_general(a, b, (((0,), (0,)), ((), ())), preferred_element_type=F32)


def dot_nt(a, b):
    return lax.dot_general(a, b, (((1,), (1,)), ((), ())), preferred_element_type=F32)


def one_hot(rows, targets):
    row = lax.broadcasted_iota(jnp.int32, (rows, targets.shape[1]), 0)
    return jnp.where(row == targets, 1.0, 0.0).astype(BF)


def in_hbm(x):
    return pltpu.with_memory_space_constraint(x, pltpu.HBM)


def call(body, outs, *args):
    return pl.pallas_call(
        body,
        out_shape=[jax.ShapeDtypeStruct(shape, dtype) for shape, dtype in outs],
        in_specs=[VMEM] * len(args),
        out_specs=[VMEM] * len(outs),
        compiler_params=PARAMS,
    )(*args)


def odd_core():
    return lax.axis_index("dom") % 2 == 1


def tree_sum(parts):
    while len(parts) > 1:
        parts = [a + b for a, b in zip(parts[::2], parts[1::2])]
    return parts[0]


def load(pairs, sems):
    copies = [pltpu.make_async_copy(a, b, sems.at[i]) for i, (a, b) in enumerate(pairs)]
    for copy in copies:
        copy.start()
    return copies


def publish_body(count, *refs):
    sources, (out_ref, *targets), sems = refs[:count], refs[count:-1], refs[-1]
    pub, rows, *rest = load(list(zip(sources, targets)), sems)
    pub_ref, features_ref = targets[:2]
    pub_count = pub_ref.shape[1]
    square = (pub_count, pub_count)
    pub.wait()
    diagonal = lax.broadcasted_iota(jnp.int32, square, 0) == lax.broadcasted_iota(jnp.int32, square, 1)
    column = jnp.sum(jnp.where(diagonal, pub_ref[...].astype(F32), 0.0), axis=1, keepdims=True)
    row = lax.broadcasted_iota(jnp.int32, (pub_count, features_ref.shape[0]), 1)
    pick = jnp.where(row == column.astype(jnp.int32), 1.0, 0.0).astype(BF)
    rows.wait()
    out_ref[...] = dot(pick, features_ref[...]).astype(BF)
    for copy in rest:
        copy.wait()


def pair_body(own_ref, other_ref, out_ref):
    rows = own_ref.shape[0]
    odd = odd_core()
    own, other = own_ref[...], other_ref[...]
    out_ref[:rows, :] = jnp.where(odd, other, own)
    out_ref[rows:, :] = jnp.where(odd, own, other)


def move_columns(bound, target, chunk, c):
    return dot_nt(bound, one_hot(chunk, target - c * chunk)).astype(BF)


def prepare_body(
    dom_size,
    pub_ref,
    features_ref,
    mask_ref,
    pos_ref,
    count_ref,
    bound_ref,
    cot_ref,
    local_ref,
    place_ref,
    target_ref,
    pick_ref,
    near_ref,
    pack_ref,
):
    pub_count = pub_ref.shape[1]
    row_count, width = features_ref.shape
    place_ref[...] = one_hot(row_count, pub_ref[...])
    me = lax.axis_index("dom")
    chip = me - me % 2
    slots = pos_ref.shape[1]
    slot_rows = slots // dom_size
    lane = lax.broadcasted_iota(jnp.int32, (1, slots), 1)
    peer = lane // slot_rows
    limit = jnp.zeros((1, slots), jnp.int32)
    for j in range(dom_size):
        limit = jnp.where(peer == j, count_ref[0:1, j : j + 1], limit)
    in_use = lane % slot_rows < limit
    target = jnp.where(in_use, (peer ^ chip) * pub_count + pos_ref[...], -1)
    target_ref[...] = target
    blocks = row_count // BLOCK
    mask = jnp.concatenate(
        [
            jnp.broadcast_to(mask_ref[0:1, b * BLOCK : (b + 1) * BLOCK].astype(F32), (HITS, BLOCK))
            for b in range(blocks)
        ],
        axis=0,
    )
    before = lax.broadcasted_iota(jnp.int32, (BLOCK, BLOCK), 0) < lax.broadcasted_iota(jnp.int32, (BLOCK, BLOCK), 1)
    rank = dot(mask.astype(BF), jnp.where(before, 1.0, 0.0).astype(BF))
    row = lax.broadcasted_iota(jnp.int32, mask.shape, 0)
    hit = jnp.where(rank == (row % HITS).astype(F32), mask, 0.0)
    pick = jnp.concatenate([jnp.where(row // HITS == b, hit, 0.0) for b in range(blocks)], axis=1).astype(BF)
    pick_ref[...] = pick
    columns = dom_size * pub_count
    features = features_ref[...]
    near = dot(pick, local_ref[...]).astype(BF)
    near_ref[...] = near
    bound = dot(pick, bound_ref[...]).astype(BF)
    pack_ref[:, columns : columns + width] = dot(pick, features)
    pack_ref[:, columns + width : columns + 2 * width] = dot(pick, cot_ref[...])
    pack_ref[:, columns + 2 * width : columns + 3 * width] = dot(near, features)
    chunk = math.gcd(columns, 512)
    ones = jnp.ones((max(chunk, row_count), width), BF)

    def move(c, total):
        block = move_columns(bound, target, chunk, c)
        pack_ref[:, pl.ds(pl.multiple_of(c * chunk, chunk), chunk)] = block.astype(F32)
        return total + dot(block, ones[:chunk])

    sums = lax.fori_loop(0, columns // chunk, move, dot(near, ones[:row_count]))
    pack_ref[:, columns + 3 * width :] = 1.0 / (1.0 + sums)


def rows_body(*refs):
    pairs, out_ref = refs[:-1], refs[-1]
    count = pairs[0].shape[0]
    for z, pair in enumerate(pairs):
        out_ref[z * count : (z + 1) * count, :] = pair[...]


def target_body(
    w_self_ref,
    w_neigh_ref,
    pack_ref,
    got_pack_ref,
    rows_ref,
    pre_ref,
    agg_ref,
    own_ref,
    total_ref,
    *messages,
):
    count = rows_ref.shape[0] // (1 + len(messages))
    odd = odd_core()
    columns, width = rows_ref.shape
    own, other = pack_ref[...], got_pack_ref[...]
    pack = jnp.concatenate([jnp.where(odd, other, own), jnp.where(odd, own, other)], axis=0)
    adj = pack[:, :columns].astype(BF)
    features, cot, part, inv = (pack[:, columns + i * width : columns + (i + 1) * width] for i in range(4))
    features = features.astype(BF)
    aggregate = ((part + dot(adj, rows_ref[...])) * inv).astype(BF)
    preact = dot(features, w_self_ref[...]) + dot(aggregate, w_neigh_ref[...])
    sigma = jax.nn.sigmoid(preact)
    slope = sigma * (1.0 + preact * (1.0 - sigma))
    grad_pre = (cot * slope).astype(BF)
    grad_agg = (dot_nt(grad_pre, w_neigh_ref[...]) * inv).astype(BF)
    pre_ref[...] = grad_pre
    agg_ref[...] = grad_agg
    total = jnp.concatenate([dot_t(features, grad_pre), dot_t(aggregate, grad_pre)], axis=0).astype(BF)
    total_ref[...] = total
    grads = dot_t(adj, grad_agg)
    own_ref[...] = grads[:count]
    for z, message in zip(range(len(messages), 0, -1), messages):
        message[:count, :] = grads[z * count : (z + 1) * count].astype(BF)
        message[count:, :] = total


def rest_body(
    features_ref,
    local_ref,
    bound_ref,
    target_ref,
    w_self_ref,
    w_neigh_ref,
    rows_ref,
    pick_ref,
    near_ref,
    pre_ref,
    agg_ref,
    hidden_ref,
    out_ref,
):
    columns, width = rows_ref.shape
    features, near = features_ref[...], local_ref[...]
    chunk = math.gcd(columns, 512)
    ones = jnp.ones((max(chunk, near.shape[1]), width), BF)

    def move(c, totals):
        block = move_columns(bound_ref[...], target_ref[...], chunk, c)
        rows = rows_ref[pl.ds(pl.multiple_of(c * chunk, chunk), chunk), :]
        return totals[0] + dot(block, rows), totals[1] + dot(block, ones[:chunk])

    start = (dot(near, features), dot(near, ones[: near.shape[1]]))
    total, sums = lax.fori_loop(0, columns // chunk, move, start)
    aggregate = (total * (1.0 / (1.0 + sums))).astype(BF)
    preact = dot(features, w_self_ref[...]) + dot(aggregate, w_neigh_ref[...])
    hidden_ref[...] = (preact * jax.nn.sigmoid(preact)).astype(BF)
    odd = odd_core()
    half = pre_ref.shape[0] // 2
    grad_pre, grad_agg = pre_ref[...], agg_ref[...]
    grad_pre = jnp.where(odd, grad_pre[half:], grad_pre[:half])
    grad_agg = jnp.where(odd, grad_agg[half:], grad_agg[:half])
    spread = dot_t(pick_ref[...], grad_pre).astype(BF)
    out_ref[...] = dot_nt(spread, w_self_ref[...]) + dot_t(near_ref[...], grad_agg)


def column_body(scale, total_ref, own_ref, *refs):
    messages, (out_ref, even_ref, odd_ref) = refs[:-3], refs[-3:]
    rows = own_ref.shape[0]
    parts = [total_ref[...]] + [message[rows:, :] for message in messages]
    out_ref[...] = (tree_sum([part.astype(F32) for part in parts]) * scale).astype(BF)
    grads = own_ref[...]
    for message in messages:
        grads = grads + message[:rows, :].astype(F32)
    even_ref[...] = grads[: rows // 2]
    odd_ref[...] = grads[rows // 2 :]


def features_body(hidden_ref, place_ref, local_grad_ref, odd_ref, even_ref, hidden_out, out_ref):
    hidden_out[...] = hidden_ref[...]
    total = jnp.where(odd_core(), odd_ref[...], even_ref[...])
    place = place_ref[...]
    high = total.astype(BF)
    low = (total - high.astype(F32)).astype(BF)
    out_ref[...] = (local_grad_ref[...] + dot(place, high) + dot(place, low)).astype(BF)


def sum_body(*refs):
    refs[-1][...] = tree_sum([part[...].astype(F32) for part in refs[:-1]])


def order_body(mine_ref, other_ref, self_ref, neigh_ref):
    total = jnp.where(odd_core(), mine_ref[...], other_ref[...])
    width = self_ref.shape[0]
    self_ref[...] = total[:width]
    neigh_ref[...] = total[width:]


def local(
    features,
    adj_local,
    adj_bound,
    w_self,
    w_neigh,
    pub_rows,
    recv_pos,
    recv_count,
    target_mask,
    cotangent,
):
    dom_size, group_size = lax.axis_size("dom"), lax.axis_size("group")
    z_size = dom_size // 2
    row_count, width = features.shape
    pub_count = pub_rows.shape[1]
    wide = (row_count, width)
    devices = range(group_size * dom_size)

    def exchange(x, odd_step, even_step):
        return lax.ppermute(x, ("group", "dom"), [(a, a ^ (odd_step if a % 2 else even_step)) for a in devices])

    def over_core(x):
        return exchange(x, 1, 1)

    first = (
        pub_rows,
        features,
        target_mask.reshape(1, row_count),
        recv_pos,
        recv_count,
        adj_bound,
        cotangent,
        adj_local,
        w_self,
        w_neigh,
    )
    published, *first = pl.pallas_call(
        functools.partial(publish_body, len(first)),
        out_shape=[jax.ShapeDtypeStruct((pub_count, width), BF)]
        + [jax.ShapeDtypeStruct(x.shape, x.dtype) for x in first],
        in_specs=[HBM] * len(first),
        out_specs=[VMEM] * (1 + len(first)),
        scratch_shapes=[pltpu.SemaphoreType.DMA((len(first),))],
        compiler_params=PARAMS,
    )(*(in_hbm(x) for x in first))
    _, features, _, _, _, adj_bound, _, adj_local, w_self, w_neigh = first
    other = over_core(published)
    columns = dom_size * pub_count
    hits = row_count // BLOCK * HITS
    place, target, pick, near, pack = call(
        functools.partial(prepare_body, dom_size),
        [
            ((row_count, pub_count), BF),
            (recv_pos.shape, jnp.int32),
            ((hits, row_count), BF),
            ((hits, row_count), BF),
            ((hits, columns + 4 * width), F32),
        ],
        *first[:8],
    )
    other, pack = lax.optimization_barrier((other, pack))
    (pair,) = call(pair_body, [((2 * pub_count, width), BF)], published, other)
    pairs = [pair] + [exchange(pair, 2 * z, 2 * z) for z in range(1, z_size)]

    square, both = (width, width), (2 * width, width)
    message = ((2 * pub_count + 2 * width, width), BF)
    (rows,) = call(rows_body, [((columns, width), BF)], *pairs)
    grad_pre, grad_agg, own_g, chip_w, *messages = call(
        target_body,
        [((2 * hits, width), BF)] * 2 + [((2 * pub_count, width), F32), (both, BF)] + [message] * (z_size - 1),
        w_self,
        w_neigh,
        pack,
        over_core(pack),
        rows,
    )
    hidden, local_grad = call(
        rest_body,
        [(wide, BF), (wide, F32)],
        features,
        adj_local,
        adj_bound,
        target,
        w_self,
        w_neigh,
        rows,
        pick,
        near,
        grad_pre,
        grad_agg,
    )
    far = range(z_size - 1, 0, -1)
    arrived = [exchange(x, 2 * z, dom_size) for z, x in zip(far, messages)][::-1]
    *arrived, hidden, local_grad = lax.optimization_barrier((*arrived, hidden, local_grad))
    scale = 1.0 / math.sqrt(row_count * group_size * dom_size // 8)
    column_w, even_g, odd_g = call(
        functools.partial(column_body, scale),
        [(both, BF)] + [((pub_count, width), F32)] * 2,
        chip_w,
        own_g,
        *arrived,
    )
    others = [exchange(column_w, dom_size * k, 2) for k in range(1, group_size)]
    *others, even_g = lax.optimization_barrier((*others, over_core(even_g)))
    hidden, grad_features = call(features_body, [(wide, BF)] * 2, hidden, place, local_grad, odd_g, even_g)
    (mine,) = call(sum_body, [(both, F32)], column_w, *others)
    grad_self, grad_neigh = call(order_body, [(square, F32)] * 2, mine, over_core(mine))
    return hidden, grad_features, grad_self, grad_neigh


def solution(mesh):
    rows = P(("group", "dom"), None)
    in_specs = (rows, rows, rows, P(), P(), rows, rows, rows, P(("group", "dom")), rows)
    return jax.shard_map(
        local, mesh=mesh, in_specs=in_specs, out_specs=(rows, rows, P(), P()), check_vma=False
    )
```

```python
import functools
import math

import jax
import jax.numpy as jnp
from jax import lax
from jax.experimental import pallas as pl
from jax.experimental.pallas import tpu as pltpu
from jax.sharding import PartitionSpec as P

BF = jnp.bfloat16
F32 = jnp.float32
BLOCK, HITS = 128, 16
VMEM = pl.BlockSpec(memory_space=pltpu.VMEM)
HBM = pl.BlockSpec(memory_space=pltpu.HBM)
PARAMS = pltpu.CompilerParams(vmem_limit_bytes=48 * 1024 * 1024)


def dot(a, b):
    return jnp.dot(a, b, preferred_element_type=F32)


def dot_t(a, b):
    return lax.dot_general(a, b, (((0,), (0,)), ((), ())), preferred_element_type=F32)


def dot_nt(a, b):
    return lax.dot_general(a, b, (((1,), (1,)), ((), ())), preferred_element_type=F32)


def one_hot(rows, targets):
    row = lax.broadcasted_iota(jnp.int32, (rows, targets.shape[1]), 0)
    return jnp.where(row == targets, 1.0, 0.0).astype(BF)


def in_hbm(x):
    return pltpu.with_memory_space_constraint(x, pltpu.HBM)


def call(body, outs, *args):
    return pl.pallas_call(
        body,
        out_shape=[jax.ShapeDtypeStruct(shape, dtype) for shape, dtype in outs],
        in_specs=[VMEM] * len(args),
        out_specs=[VMEM] * len(outs),
        compiler_params=PARAMS,
    )(*args)


def odd_core():
    return lax.axis_index("dom") % 2 == 1


def tree_sum(parts):
    while len(parts) > 1:
        parts = [a + b for a, b in zip(parts[::2], parts[1::2])]
    return parts[0]


def load(pairs, sems):
    copies = [pltpu.make_async_copy(a, b, sems.at[i]) for i, (a, b) in enumerate(pairs)]
    for copy in copies:
        copy.start()
    return copies


def publish_body(count, *refs):
    sources, (out_ref, *targets), sems = refs[:count], refs[count:-1], refs[-1]
    pub, rows, *rest = load(list(zip(sources, targets)), sems)
    pub_ref, features_ref = targets[:2]
    pub_count = pub_ref.shape[1]
    square = (pub_count, pub_count)
    pub.wait()
    diagonal = lax.broadcasted_iota(jnp.int32, square, 0) == lax.broadcasted_iota(jnp.int32, square, 1)
    column = jnp.sum(jnp.where(diagonal, pub_ref[...].astype(F32), 0.0), axis=1, keepdims=True)
    row = lax.broadcasted_iota(jnp.int32, (pub_count, features_ref.shape[0]), 1)
    pick = jnp.where(row == column.astype(jnp.int32), 1.0, 0.0).astype(BF)
    rows.wait()
    out_ref[...] = dot(pick, features_ref[...]).astype(BF)
    for copy in rest:
        copy.wait()


def pair_body(own_ref, other_ref, out_ref):
    rows = own_ref.shape[0]
    odd = odd_core()
    own, other = own_ref[...], other_ref[...]
    out_ref[:rows, :] = jnp.where(odd, other, own)
    out_ref[rows:, :] = jnp.where(odd, own, other)


def move_columns(bound, target, chunk, c):
    return dot_nt(bound, one_hot(chunk, target - c * chunk)).astype(BF)


def prepare_body(
    dom_size,
    pub_ref,
    features_ref,
    mask_ref,
    pos_ref,
    count_ref,
    bound_ref,
    cot_ref,
    local_ref,
    place_ref,
    target_ref,
    pick_ref,
    near_ref,
    pack_ref,
):
    pub_count = pub_ref.shape[1]
    row_count, width = features_ref.shape
    place_ref[...] = one_hot(row_count, pub_ref[...])
    me = lax.axis_index("dom")
    chip = me - me % 2
    slots = pos_ref.shape[1]
    slot_rows = slots // dom_size
    lane = lax.broadcasted_iota(jnp.int32, (1, slots), 1)
    peer = lane // slot_rows
    limit = jnp.zeros((1, slots), jnp.int32)
    for j in range(dom_size):
        limit = jnp.where(peer == j, count_ref[0:1, j : j + 1], limit)
    in_use = lane % slot_rows < limit
    target = jnp.where(in_use, (peer ^ chip) * pub_count + pos_ref[...], -1)
    target_ref[...] = target
    blocks = row_count // BLOCK
    mask = jnp.concatenate(
        [
            jnp.broadcast_to(mask_ref[0:1, b * BLOCK : (b + 1) * BLOCK].astype(F32), (HITS, BLOCK))
            for b in range(blocks)
        ],
        axis=0,
    )
    before = lax.broadcasted_iota(jnp.int32, (BLOCK, BLOCK), 0) < lax.broadcasted_iota(jnp.int32, (BLOCK, BLOCK), 1)
    rank = dot(mask.astype(BF), jnp.where(before, 1.0, 0.0).astype(BF))
    row = lax.broadcasted_iota(jnp.int32, mask.shape, 0)
    hit = jnp.where(rank == (row % HITS).astype(F32), mask, 0.0)
    pick = jnp.concatenate([jnp.where(row // HITS == b, hit, 0.0) for b in range(blocks)], axis=1).astype(BF)
    pick_ref[...] = pick
    columns = dom_size * pub_count
    features = features_ref[...]
    near = dot(pick, local_ref[...]).astype(BF)
    near_ref[...] = near
    bound = dot(pick, bound_ref[...]).astype(BF)
    pack_ref[:, columns : columns + width] = dot(pick, features)
    pack_ref[:, columns + width : columns + 2 * width] = dot(pick, cot_ref[...])
    pack_ref[:, columns + 2 * width : columns + 3 * width] = dot(near, features)
    chunk = math.gcd(columns, 512)
    ones = jnp.ones((max(chunk, row_count), width), BF)

    def move(c, total):
        block = move_columns(bound, target, chunk, c)
        pack_ref[:, pl.ds(pl.multiple_of(c * chunk, chunk), chunk)] = block.astype(F32)
        return total + dot(block, ones[:chunk])

    sums = lax.fori_loop(0, columns // chunk, move, dot(near, ones[:row_count]))
    pack_ref[:, columns + 3 * width :] = 1.0 / (1.0 + sums)


def rows_body(*refs):
    pairs, out_ref = refs[:-1], refs[-1]
    count = pairs[0].shape[0]
    for z, pair in enumerate(pairs):
        out_ref[z * count : (z + 1) * count, :] = pair[...]


def target_body(
    w_self_ref,
    w_neigh_ref,
    pack_ref,
    got_pack_ref,
    rows_ref,
    pre_ref,
    agg_ref,
    own_ref,
    total_ref,
    *messages,
):
    count = rows_ref.shape[0] // (1 + len(messages))
    odd = odd_core()
    columns, width = rows_ref.shape
    own, other = pack_ref[...], got_pack_ref[...]
    pack = jnp.concatenate([jnp.where(odd, other, own), jnp.where(odd, own, other)], axis=0)
    adj = pack[:, :columns].astype(BF)
    features, cot, part, inv = (pack[:, columns + i * width : columns + (i + 1) * width] for i in range(4))
    features = features.astype(BF)
    aggregate = ((part + dot(adj, rows_ref[...])) * inv).astype(BF)
    preact = dot(features, w_self_ref[...]) + dot(aggregate, w_neigh_ref[...])
    sigma = jax.nn.sigmoid(preact)
    slope = sigma * (1.0 + preact * (1.0 - sigma))
    grad_pre = (cot * slope).astype(BF)
    grad_agg = (dot_nt(grad_pre, w_neigh_ref[...]) * inv).astype(BF)
    pre_ref[...] = grad_pre
    agg_ref[...] = grad_agg
    total = jnp.concatenate([dot_t(features, grad_pre), dot_t(aggregate, grad_pre)], axis=0).astype(BF)
    total_ref[...] = total
    grads = dot_t(adj, grad_agg)
    own_ref[...] = grads[:count]
    for z, message in zip(range(len(messages), 0, -1), messages):
        message[:count, :] = grads[z * count : (z + 1) * count].astype(BF)
        message[count:, :] = total


def rest_body(
    features_ref,
    local_ref,
    bound_ref,
    target_ref,
    w_self_ref,
    w_neigh_ref,
    rows_ref,
    pick_ref,
    near_ref,
    pre_ref,
    agg_ref,
    hidden_ref,
    out_ref,
):
    columns, width = rows_ref.shape
    features, near = features_ref[...], local_ref[...]
    chunk = math.gcd(columns, 512)
    ones = jnp.ones((max(chunk, near.shape[1]), width), BF)

    def move(c, totals):
        block = move_columns(bound_ref[...], target_ref[...], chunk, c)
        rows = rows_ref[pl.ds(pl.multiple_of(c * chunk, chunk), chunk), :]
        return totals[0] + dot(block, rows), totals[1] + dot(block, ones[:chunk])

    start = (dot(near, features), dot(near, ones[: near.shape[1]]))
    total, sums = lax.fori_loop(0, columns // chunk, move, start)
    aggregate = (total * (1.0 / (1.0 + sums))).astype(BF)
    preact = dot(features, w_self_ref[...]) + dot(aggregate, w_neigh_ref[...])
    hidden_ref[...] = (preact * jax.nn.sigmoid(preact)).astype(BF)
    odd = odd_core()
    half = pre_ref.shape[0] // 2
    grad_pre, grad_agg = pre_ref[...], agg_ref[...]
    grad_pre = jnp.where(odd, grad_pre[half:], grad_pre[:half])
    grad_agg = jnp.where(odd, grad_agg[half:], grad_agg[:half])
    spread = dot_t(pick_ref[...], grad_pre).astype(BF)
    out_ref[...] = dot_nt(spread, w_self_ref[...]) + dot_t(near_ref[...], grad_agg)


def column_body(scale, total_ref, own_ref, *refs):
    messages, (out_ref, even_ref, odd_ref) = refs[:-3], refs[-3:]
    rows = own_ref.shape[0]
    parts = [total_ref[...]] + [message[rows:, :] for message in messages]
    out_ref[...] = (tree_sum([part.astype(F32) for part in parts]) * scale).astype(BF)
    grads = own_ref[...]
    for message in messages:
        grads = grads + message[:rows, :].astype(F32)
    even_ref[...] = grads[: rows // 2]
    odd_ref[...] = grads[rows // 2 :]


def features_body(hidden_ref, place_ref, local_grad_ref, odd_ref, even_ref, hidden_out, out_ref):
    hidden_out[...] = hidden_ref[...]
    total = jnp.where(odd_core(), odd_ref[...], even_ref[...])
    place = place_ref[...]
    high = total.astype(BF)
    low = (total - high.astype(F32)).astype(BF)
    out_ref[...] = (local_grad_ref[...] + dot(place, high) + dot(place, low)).astype(BF)


def sum_body(*refs):
    refs[-1][...] = tree_sum([part[...].astype(F32) for part in refs[:-1]])


def order_body(mine_ref, other_ref, self_ref, neigh_ref):
    total = jnp.where(odd_core(), mine_ref[...], other_ref[...])
    width = self_ref.shape[0]
    self_ref[...] = total[:width]
    neigh_ref[...] = total[width:]


def local(
    features,
    adj_local,
    adj_bound,
    w_self,
    w_neigh,
    pub_rows,
    recv_pos,
    recv_count,
    target_mask,
    cotangent,
):
    dom_size, group_size = lax.axis_size("dom"), lax.axis_size("group")
    z_size = dom_size // 2
    row_count, width = features.shape
    pub_count = pub_rows.shape[1]
    wide = (row_count, width)
    devices = range(group_size * dom_size)

    def exchange(x, odd_step, even_step):
        return lax.ppermute(x, ("group", "dom"), [(a, a ^ (odd_step if a % 2 else even_step)) for a in devices])

    def over_core(x):
        return exchange(x, 1, 1)

    first = (
        pub_rows,
        features,
        target_mask.reshape(1, row_count),
        recv_pos,
        recv_count,
        adj_bound,
        cotangent,
        adj_local,
        w_self,
        w_neigh,
    )
    published, *first = pl.pallas_call(
        functools.partial(publish_body, len(first)),
        out_shape=[jax.ShapeDtypeStruct((pub_count, width), BF)]
        + [jax.ShapeDtypeStruct(x.shape, x.dtype) for x in first],
        in_specs=[HBM] * len(first),
        out_specs=[VMEM] * (1 + len(first)),
        scratch_shapes=[pltpu.SemaphoreType.DMA((len(first),))],
        compiler_params=PARAMS,
    )(*(in_hbm(x) for x in first))
    _, features, _, _, _, adj_bound, _, adj_local, w_self, w_neigh = first
    other = over_core(published)
    columns = dom_size * pub_count
    hits = row_count // BLOCK * HITS
    place, target, pick, near, pack = call(
        functools.partial(prepare_body, dom_size),
        [
            ((row_count, pub_count), BF),
            (recv_pos.shape, jnp.int32),
            ((hits, row_count), BF),
            ((hits, row_count), BF),
            ((hits, columns + 4 * width), F32),
        ],
        *first[:8],
    )
    other, pack = lax.optimization_barrier((other, pack))
    (pair,) = call(pair_body, [((2 * pub_count, width), BF)], published, other)
    pairs = [pair] + [exchange(pair, 2 * z, 2 * z) for z in range(1, z_size)]

    square, both = (width, width), (2 * width, width)
    message = ((2 * pub_count + 2 * width, width), BF)
    (rows,) = call(rows_body, [((columns, width), BF)], *pairs)
    grad_pre, grad_agg, own_g, chip_w, *messages = call(
        target_body,
        [((2 * hits, width), BF)] * 2 + [((2 * pub_count, width), F32), (both, BF)] + [message] * (z_size - 1),
        w_self,
        w_neigh,
        pack,
        over_core(pack),
        rows,
    )
    hidden, local_grad = call(
        rest_body,
        [(wide, BF), (wide, F32)],
        features,
        adj_local,
        adj_bound,
        target,
        w_self,
        w_neigh,
        rows,
        pick,
        near,
        grad_pre,
        grad_agg,
    )
    far = range(z_size - 1, 0, -1)
    arrived = [exchange(x, 2 * z, dom_size) for z, x in zip(far, messages)][::-1]
    *arrived, hidden, local_grad = lax.optimization_barrier((*arrived, hidden, local_grad))
    scale = 1.0 / math.sqrt(row_count * group_size * dom_size // 8)
    column_w, even_g, odd_g = call(
        functools.partial(column_body, scale),
        [(both, BF)] + [((pub_count, width), F32)] * 2,
        chip_w,
        own_g,
        *arrived,
    )
    others = [exchange(column_w, dom_size * k, 2 if k % 2 else dom_size) for k in range(1, group_size)]
    *others, even_g = lax.optimization_barrier((*others, over_core(even_g)))
    hidden, grad_features = call(features_body, [(wide, BF)] * 2, hidden, place, local_grad, odd_g, even_g)
    (mine,) = call(sum_body, [(both, F32)], column_w, *others)
    grad_self, grad_neigh = call(order_body, [(square, F32)] * 2, mine, over_core(mine))
    return hidden, grad_features, grad_self, grad_neigh


def solution(mesh):
    rows = P(("group", "dom"), None)
    in_specs = (rows, rows, rows, P(), P(), rows, rows, rows, P(("group", "dom")), rows)
    return jax.shard_map(
        local, mesh=mesh, in_specs=in_specs, out_specs=(rows, rows, P(), P()), check_vma=False
    )
```

```python
import functools
import math

import jax
import jax.numpy as jnp
from jax import lax
from jax.experimental import pallas as pl
from jax.experimental.pallas import tpu as pltpu
from jax.sharding import PartitionSpec as P

BF = jnp.bfloat16
F32 = jnp.float32
BLOCK, HITS = 128, 16
VMEM = pl.BlockSpec(memory_space=pltpu.VMEM)
HBM = pl.BlockSpec(memory_space=pltpu.HBM)
PARAMS = pltpu.CompilerParams(vmem_limit_bytes=48 * 1024 * 1024)


def dot(a, b):
    return jnp.dot(a, b, preferred_element_type=F32)


def dot_t(a, b):
    return lax.dot_general(a, b, (((0,), (0,)), ((), ())), preferred_element_type=F32)


def dot_nt(a, b):
    return lax.dot_general(a, b, (((1,), (1,)), ((), ())), preferred_element_type=F32)


def one_hot(rows, targets):
    row = lax.broadcasted_iota(jnp.int32, (rows, targets.shape[1]), 0)
    return jnp.where(row == targets, 1.0, 0.0).astype(BF)


def in_hbm(x):
    return pltpu.with_memory_space_constraint(x, pltpu.HBM)


def call(body, outs, *args):
    return pl.pallas_call(
        body,
        out_shape=[jax.ShapeDtypeStruct(shape, dtype) for shape, dtype in outs],
        in_specs=[VMEM] * len(args),
        out_specs=[VMEM] * len(outs),
        compiler_params=PARAMS,
    )(*args)


def odd_core():
    return lax.axis_index("dom") % 2 == 1


def tree_sum(parts):
    while len(parts) > 1:
        parts = [a + b for a, b in zip(parts[::2], parts[1::2])]
    return parts[0]


def load(pairs, sems):
    copies = [pltpu.make_async_copy(a, b, sems.at[i]) for i, (a, b) in enumerate(pairs)]
    for copy in copies:
        copy.start()
    return copies


def publish_body(count, *refs):
    sources, (out_ref, *targets), sems = refs[:count], refs[count:-1], refs[-1]
    pub, rows, *rest = load(list(zip(sources, targets)), sems)
    pub_ref, features_ref = targets[:2]
    pub_count = pub_ref.shape[1]
    square = (pub_count, pub_count)
    pub.wait()
    diagonal = lax.broadcasted_iota(jnp.int32, square, 0) == lax.broadcasted_iota(jnp.int32, square, 1)
    column = jnp.sum(jnp.where(diagonal, pub_ref[...].astype(F32), 0.0), axis=1, keepdims=True)
    row = lax.broadcasted_iota(jnp.int32, (pub_count, features_ref.shape[0]), 1)
    pick = jnp.where(row == column.astype(jnp.int32), 1.0, 0.0).astype(BF)
    rows.wait()
    out_ref[...] = dot(pick, features_ref[...]).astype(BF)
    for copy in rest:
        copy.wait()


def pair_body(own_ref, other_ref, out_ref):
    rows = own_ref.shape[0]
    odd = odd_core()
    own, other = own_ref[...], other_ref[...]
    out_ref[:rows, :] = jnp.where(odd, other, own)
    out_ref[rows:, :] = jnp.where(odd, own, other)


def move_columns(bound, target, chunk, c):
    return dot_nt(bound, one_hot(chunk, target - c * chunk)).astype(BF)


def prepare_body(
    dom_size,
    pub_ref,
    features_ref,
    mask_ref,
    pos_ref,
    count_ref,
    bound_ref,
    cot_ref,
    local_ref,
    place_ref,
    target_ref,
    pick_ref,
    near_ref,
    pack_ref,
):
    pub_count = pub_ref.shape[1]
    row_count, width = features_ref.shape
    place_ref[...] = one_hot(row_count, pub_ref[...])
    me = lax.axis_index("dom")
    chip = me - me % 2
    slots = pos_ref.shape[1]
    slot_rows = slots // dom_size
    lane = lax.broadcasted_iota(jnp.int32, (1, slots), 1)
    peer = lane // slot_rows
    limit = jnp.zeros((1, slots), jnp.int32)
    for j in range(dom_size):
        limit = jnp.where(peer == j, count_ref[0:1, j : j + 1], limit)
    in_use = lane % slot_rows < limit
    target = jnp.where(in_use, (peer ^ chip) * pub_count + pos_ref[...], -1)
    target_ref[...] = target
    blocks = row_count // BLOCK
    mask = jnp.concatenate(
        [
            jnp.broadcast_to(mask_ref[0:1, b * BLOCK : (b + 1) * BLOCK].astype(F32), (HITS, BLOCK))
            for b in range(blocks)
        ],
        axis=0,
    )
    before = lax.broadcasted_iota(jnp.int32, (BLOCK, BLOCK), 0) < lax.broadcasted_iota(jnp.int32, (BLOCK, BLOCK), 1)
    rank = dot(mask.astype(BF), jnp.where(before, 1.0, 0.0).astype(BF))
    row = lax.broadcasted_iota(jnp.int32, mask.shape, 0)
    hit = jnp.where(rank == (row % HITS).astype(F32), mask, 0.0)
    pick = jnp.concatenate([jnp.where(row // HITS == b, hit, 0.0) for b in range(blocks)], axis=1).astype(BF)
    pick_ref[...] = pick
    columns = dom_size * pub_count
    features = features_ref[...]
    near = dot(pick, local_ref[...]).astype(BF)
    near_ref[...] = near
    bound = dot(pick, bound_ref[...]).astype(BF)
    pack_ref[:, columns : columns + width] = dot(pick, features)
    pack_ref[:, columns + width : columns + 2 * width] = dot(pick, cot_ref[...])
    pack_ref[:, columns + 2 * width : columns + 3 * width] = dot(near, features)
    chunk = math.gcd(columns, 512)
    ones = jnp.ones((max(chunk, row_count), width), BF)

    def move(c, total):
        block = move_columns(bound, target, chunk, c)
        pack_ref[:, pl.ds(pl.multiple_of(c * chunk, chunk), chunk)] = block.astype(F32)
        return total + dot(block, ones[:chunk])

    sums = lax.fori_loop(0, columns // chunk, move, dot(near, ones[:row_count]))
    pack_ref[:, columns + 3 * width :] = 1.0 / (1.0 + sums)


def rows_body(*refs):
    pairs, out_ref = refs[:-1], refs[-1]
    count = pairs[0].shape[0]
    for z, pair in enumerate(pairs):
        out_ref[z * count : (z + 1) * count, :] = pair[...]


def target_body(
    w_self_ref,
    w_neigh_ref,
    pack_ref,
    got_pack_ref,
    rows_ref,
    pre_ref,
    agg_ref,
    own_ref,
    total_ref,
    *messages,
):
    count = rows_ref.shape[0] // (1 + len(messages))
    odd = odd_core()
    columns, width = rows_ref.shape
    own, other = pack_ref[...], got_pack_ref[...]
    pack = jnp.concatenate([jnp.where(odd, other, own), jnp.where(odd, own, other)], axis=0)
    adj = pack[:, :columns].astype(BF)
    features, cot, part, inv = (pack[:, columns + i * width : columns + (i + 1) * width] for i in range(4))
    features = features.astype(BF)
    aggregate = ((part + dot(adj, rows_ref[...])) * inv).astype(BF)
    preact = dot(features, w_self_ref[...]) + dot(aggregate, w_neigh_ref[...])
    sigma = jax.nn.sigmoid(preact)
    slope = sigma * (1.0 + preact * (1.0 - sigma))
    grad_pre = (cot * slope).astype(BF)
    grad_agg = (dot_nt(grad_pre, w_neigh_ref[...]) * inv).astype(BF)
    pre_ref[...] = grad_pre
    agg_ref[...] = grad_agg
    total = jnp.concatenate([dot_t(features, grad_pre), dot_t(aggregate, grad_pre)], axis=0).astype(BF)
    total_ref[...] = total
    grads = dot_t(adj, grad_agg)
    own_ref[...] = grads[:count]
    for z, message in zip(range(len(messages), 0, -1), messages):
        message[:count, :] = grads[z * count : (z + 1) * count].astype(BF)
        message[count:, :] = total


def rest_body(
    features_ref,
    local_ref,
    bound_ref,
    target_ref,
    w_self_ref,
    w_neigh_ref,
    rows_ref,
    pick_ref,
    near_ref,
    pre_ref,
    agg_ref,
    hidden_ref,
    out_ref,
):
    columns, width = rows_ref.shape
    features, near = features_ref[...], local_ref[...]
    chunk = math.gcd(columns, 512)
    ones = jnp.ones((max(chunk, near.shape[1]), width), BF)

    def move(c, totals):
        block = move_columns(bound_ref[...], target_ref[...], chunk, c)
        rows = rows_ref[pl.ds(pl.multiple_of(c * chunk, chunk), chunk), :]
        return totals[0] + dot(block, rows), totals[1] + dot(block, ones[:chunk])

    start = (dot(near, features), dot(near, ones[: near.shape[1]]))
    total, sums = lax.fori_loop(0, columns // chunk, move, start)
    aggregate = (total * (1.0 / (1.0 + sums))).astype(BF)
    preact = dot(features, w_self_ref[...]) + dot(aggregate, w_neigh_ref[...])
    hidden_ref[...] = (preact * jax.nn.sigmoid(preact)).astype(BF)
    odd = odd_core()
    half = pre_ref.shape[0] // 2
    grad_pre, grad_agg = pre_ref[...], agg_ref[...]
    grad_pre = jnp.where(odd, grad_pre[half:], grad_pre[:half])
    grad_agg = jnp.where(odd, grad_agg[half:], grad_agg[:half])
    spread = dot_t(pick_ref[...], grad_pre).astype(BF)
    out_ref[...] = dot_nt(spread, w_self_ref[...]) + dot_t(near_ref[...], grad_agg)


def column_body(scale, total_ref, own_ref, *refs):
    messages, (out_ref, even_ref, odd_ref) = refs[:-3], refs[-3:]
    rows = own_ref.shape[0]
    parts = [total_ref[...]] + [message[rows:, :] for message in messages]
    out_ref[...] = (tree_sum([part.astype(F32) for part in parts]) * scale).astype(BF)
    grads = own_ref[...]
    for message in messages:
        grads = grads + message[:rows, :].astype(F32)
    even_ref[...] = grads[: rows // 2]
    odd_ref[...] = grads[rows // 2 :]


def features_body(hidden_ref, place_ref, local_grad_ref, odd_ref, even_ref, hidden_out, out_ref):
    hidden_out[...] = hidden_ref[...]
    total = jnp.where(odd_core(), odd_ref[...], even_ref[...])
    place = place_ref[...]
    high = total.astype(BF)
    low = (total - high.astype(F32)).astype(BF)
    out_ref[...] = (local_grad_ref[...] + dot(place, high) + dot(place, low)).astype(BF)


def sum_body(*refs):
    refs[-1][...] = tree_sum([part[...].astype(F32) for part in refs[:-1]])


def order_body(mine_ref, other_ref, self_ref, neigh_ref):
    total = jnp.where(odd_core(), mine_ref[...], other_ref[...])
    width = self_ref.shape[0]
    self_ref[...] = total[:width]
    neigh_ref[...] = total[width:]


def local(
    features,
    adj_local,
    adj_bound,
    w_self,
    w_neigh,
    pub_rows,
    recv_pos,
    recv_count,
    target_mask,
    cotangent,
):
    dom_size, group_size = lax.axis_size("dom"), lax.axis_size("group")
    z_size = dom_size // 2
    row_count, width = features.shape
    pub_count = pub_rows.shape[1]
    wide = (row_count, width)
    devices = range(group_size * dom_size)

    def exchange(x, odd_step, even_step):
        return lax.ppermute(x, ("group", "dom"), [(a, a ^ (odd_step if a % 2 else even_step)) for a in devices])

    def over_core(x):
        return exchange(x, 1, 1)

    first = (
        pub_rows,
        features,
        target_mask.reshape(1, row_count),
        recv_pos,
        recv_count,
        adj_bound,
        cotangent,
        adj_local,
        w_self,
        w_neigh,
    )
    published, *first = pl.pallas_call(
        functools.partial(publish_body, len(first)),
        out_shape=[jax.ShapeDtypeStruct((pub_count, width), BF)]
        + [jax.ShapeDtypeStruct(x.shape, x.dtype) for x in first],
        in_specs=[HBM] * len(first),
        out_specs=[VMEM] * (1 + len(first)),
        scratch_shapes=[pltpu.SemaphoreType.DMA((len(first),))],
        compiler_params=PARAMS,
    )(*(in_hbm(x) for x in first))
    _, features, _, _, _, adj_bound, _, adj_local, w_self, w_neigh = first
    other = over_core(published)
    columns = dom_size * pub_count
    hits = row_count // BLOCK * HITS
    place, target, pick, near, pack = call(
        functools.partial(prepare_body, dom_size),
        [
            ((row_count, pub_count), BF),
            (recv_pos.shape, jnp.int32),
            ((hits, row_count), BF),
            ((hits, row_count), BF),
            ((hits, columns + 4 * width), F32),
        ],
        *first[:8],
    )
    other, pack = lax.optimization_barrier((other, pack))
    (pair,) = call(pair_body, [((2 * pub_count, width), BF)], published, other)
    pairs = [pair] + [exchange(pair, 2 * z + 1, 2 * z + 1) for z in range(1, z_size)]

    square, both = (width, width), (2 * width, width)
    message = ((2 * pub_count + 2 * width, width), BF)
    (rows,) = call(rows_body, [((columns, width), BF)], *pairs)
    grad_pre, grad_agg, own_g, chip_w, *messages = call(
        target_body,
        [((2 * hits, width), BF)] * 2 + [((2 * pub_count, width), F32), (both, BF)] + [message] * (z_size - 1),
        w_self,
        w_neigh,
        pack,
        over_core(pack),
        rows,
    )
    hidden, local_grad = call(
        rest_body,
        [(wide, BF), (wide, F32)],
        features,
        adj_local,
        adj_bound,
        target,
        w_self,
        w_neigh,
        rows,
        pick,
        near,
        grad_pre,
        grad_agg,
    )
    far = range(z_size - 1, 0, -1)
    arrived = [exchange(x, 2 * z, dom_size) for z, x in zip(far, messages)][::-1]
    *arrived, hidden, local_grad = lax.optimization_barrier((*arrived, hidden, local_grad))
    scale = 1.0 / math.sqrt(row_count * group_size * dom_size // 8)
    column_w, even_g, odd_g = call(
        functools.partial(column_body, scale),
        [(both, BF)] + [((pub_count, width), F32)] * 2,
        chip_w,
        own_g,
        *arrived,
    )
    others = [exchange(column_w, dom_size * k, 2 if k % 2 else dom_size) for k in range(1, group_size)]
    *others, even_g = lax.optimization_barrier((*others, over_core(even_g)))
    hidden, grad_features = call(features_body, [(wide, BF)] * 2, hidden, place, local_grad, odd_g, even_g)
    (mine,) = call(sum_body, [(both, F32)], column_w, *others)
    grad_self, grad_neigh = call(order_body, [(square, F32)] * 2, mine, over_core(mine))
    return hidden, grad_features, grad_self, grad_neigh


def solution(mesh):
    rows = P(("group", "dom"), None)
    in_specs = (rows, rows, rows, P(), P(), rows, rows, rows, P(("group", "dom")), rows)
    return jax.shard_map(
        local, mesh=mesh, in_specs=in_specs, out_specs=(rows, rows, P(), P()), check_vma=False
    )
```

```python
import functools
import math

import jax
import jax.numpy as jnp
from jax import lax
from jax.experimental import pallas as pl
from jax.experimental.pallas import tpu as pltpu
from jax.sharding import PartitionSpec as P

BF = jnp.bfloat16
F32 = jnp.float32
BLOCK, HITS = 128, 16
VMEM = pl.BlockSpec(memory_space=pltpu.VMEM)
HBM = pl.BlockSpec(memory_space=pltpu.HBM)
PARAMS = pltpu.CompilerParams(vmem_limit_bytes=48 * 1024 * 1024)


def dot(a, b):
    return jnp.dot(a, b, preferred_element_type=F32)


def dot_t(a, b):
    return lax.dot_general(a, b, (((0,), (0,)), ((), ())), preferred_element_type=F32)


def dot_nt(a, b):
    return lax.dot_general(a, b, (((1,), (1,)), ((), ())), preferred_element_type=F32)


def one_hot(rows, targets):
    row = lax.broadcasted_iota(jnp.int32, (rows, targets.shape[1]), 0)
    return jnp.where(row == targets, 1.0, 0.0).astype(BF)


def in_hbm(x):
    return pltpu.with_memory_space_constraint(x, pltpu.HBM)


def call(body, outs, *args):
    return pl.pallas_call(
        body,
        out_shape=[jax.ShapeDtypeStruct(shape, dtype) for shape, dtype in outs],
        in_specs=[VMEM] * len(args),
        out_specs=[VMEM] * len(outs),
        compiler_params=PARAMS,
    )(*args)


def odd_core():
    return lax.axis_index("dom") % 2 == 1


def tree_sum(parts):
    while len(parts) > 1:
        parts = [a + b for a, b in zip(parts[::2], parts[1::2])]
    return parts[0]


def load(pairs, sems):
    copies = [pltpu.make_async_copy(a, b, sems.at[i]) for i, (a, b) in enumerate(pairs)]
    for copy in copies:
        copy.start()
    return copies


def publish_body(count, *refs):
    sources, (out_ref, *targets), sems = refs[:count], refs[count:-1], refs[-1]
    pub, rows, *rest = load(list(zip(sources, targets)), sems)
    pub_ref, features_ref = targets[:2]
    pub_count = pub_ref.shape[1]
    square = (pub_count, pub_count)
    pub.wait()
    diagonal = lax.broadcasted_iota(jnp.int32, square, 0) == lax.broadcasted_iota(jnp.int32, square, 1)
    column = jnp.sum(jnp.where(diagonal, pub_ref[...].astype(F32), 0.0), axis=1, keepdims=True)
    row = lax.broadcasted_iota(jnp.int32, (pub_count, features_ref.shape[0]), 1)
    pick = jnp.where(row == column.astype(jnp.int32), 1.0, 0.0).astype(BF)
    rows.wait()
    out_ref[...] = dot(pick, features_ref[...]).astype(BF)
    for copy in rest:
        copy.wait()


def pair_body(own_ref, other_ref, out_ref):
    rows = own_ref.shape[0]
    odd = odd_core()
    own, other = own_ref[...], other_ref[...]
    out_ref[:rows, :] = jnp.where(odd, other, own)
    out_ref[rows:, :] = jnp.where(odd, own, other)


def move_columns(bound, target, chunk, c):
    return dot_nt(bound, one_hot(chunk, target - c * chunk)).astype(BF)


def prepare_body(
    dom_size,
    pub_ref,
    features_ref,
    mask_ref,
    pos_ref,
    count_ref,
    bound_ref,
    cot_ref,
    local_ref,
    place_ref,
    target_ref,
    pick_ref,
    near_ref,
    pack_ref,
):
    pub_count = pub_ref.shape[1]
    row_count, width = features_ref.shape
    place_ref[...] = one_hot(row_count, pub_ref[...])
    me = lax.axis_index("dom")
    chip = me - me % 2
    slots = pos_ref.shape[1]
    slot_rows = slots // dom_size
    lane = lax.broadcasted_iota(jnp.int32, (1, slots), 1)
    peer = lane // slot_rows
    limit = jnp.zeros((1, slots), jnp.int32)
    for j in range(dom_size):
        limit = jnp.where(peer == j, count_ref[0:1, j : j + 1], limit)
    in_use = lane % slot_rows < limit
    target = jnp.where(in_use, (peer ^ chip) * pub_count + pos_ref[...], -1)
    target_ref[...] = target
    blocks = row_count // BLOCK
    mask = jnp.concatenate(
        [
            jnp.broadcast_to(mask_ref[0:1, b * BLOCK : (b + 1) * BLOCK].astype(F32), (HITS, BLOCK))
            for b in range(blocks)
        ],
        axis=0,
    )
    before = lax.broadcasted_iota(jnp.int32, (BLOCK, BLOCK), 0) < lax.broadcasted_iota(jnp.int32, (BLOCK, BLOCK), 1)
    rank = dot(mask.astype(BF), jnp.where(before, 1.0, 0.0).astype(BF))
    row = lax.broadcasted_iota(jnp.int32, mask.shape, 0)
    hit = jnp.where(rank == (row % HITS).astype(F32), mask, 0.0)
    pick = jnp.concatenate([jnp.where(row // HITS == b, hit, 0.0) for b in range(blocks)], axis=1).astype(BF)
    pick_ref[...] = pick
    columns = dom_size * pub_count
    features = features_ref[...]
    near = dot(pick, local_ref[...]).astype(BF)
    near_ref[...] = near
    bound = dot(pick, bound_ref[...]).astype(BF)
    pack_ref[:, columns : columns + width] = dot(pick, features)
    pack_ref[:, columns + width : columns + 2 * width] = dot(pick, cot_ref[...])
    pack_ref[:, columns + 2 * width : columns + 3 * width] = dot(near, features)
    chunk = math.gcd(columns, 512)
    ones = jnp.ones((max(chunk, row_count), width), BF)

    def move(c, total):
        block = move_columns(bound, target, chunk, c)
        pack_ref[:, pl.ds(pl.multiple_of(c * chunk, chunk), chunk)] = block.astype(F32)
        return total + dot(block, ones[:chunk])

    sums = lax.fori_loop(0, columns // chunk, move, dot(near, ones[:row_count]))
    pack_ref[:, columns + 3 * width :] = 1.0 / (1.0 + sums)


def either(mine, others):
    odd = odd_core()
    pairs = [(a[...], b[...]) for a, b in zip(mine, others)]
    return [jnp.where(odd, a, b) for a, b in pairs] + [jnp.where(odd, b, a) for a, b in pairs]


def by_peer(peers, own, refs):
    near, *far = peers
    count = len(far) // 2
    parts = dict(zip(far, either(refs[1 : 1 + count], refs[1 + count : 1 + 2 * count])))
    parts |= {0: own, near: refs[0][...]}
    return [parts[k] for k in sorted(parts)]


def rows_body(peers, pair_ref, *refs):
    refs, out_ref = refs[:-1], refs[-1]
    count = pair_ref.shape[0]
    for z, pair in enumerate(by_peer(peers, pair_ref[...], refs)):
        out_ref[z * count : (z + 1) * count, :] = pair


def target_body(
    peers,
    w_self_ref,
    w_neigh_ref,
    pack_ref,
    got_pack_ref,
    rows_ref,
    pre_ref,
    agg_ref,
    own_ref,
    total_ref,
    *messages,
):
    count = rows_ref.shape[0] // (1 + len(peers))
    odd = odd_core()
    columns, width = rows_ref.shape
    own, other = pack_ref[...], got_pack_ref[...]
    pack = jnp.concatenate([jnp.where(odd, other, own), jnp.where(odd, own, other)], axis=0)
    adj = pack[:, :columns].astype(BF)
    features, cot, part, inv = (pack[:, columns + i * width : columns + (i + 1) * width] for i in range(4))
    features = features.astype(BF)
    aggregate = ((part + dot(adj, rows_ref[...])) * inv).astype(BF)
    preact = dot(features, w_self_ref[...]) + dot(aggregate, w_neigh_ref[...])
    sigma = jax.nn.sigmoid(preact)
    slope = sigma * (1.0 + preact * (1.0 - sigma))
    grad_pre = (cot * slope).astype(BF)
    grad_agg = (dot_nt(grad_pre, w_neigh_ref[...]) * inv).astype(BF)
    pre_ref[...] = grad_pre
    agg_ref[...] = grad_agg
    total = jnp.concatenate([dot_t(features, grad_pre), dot_t(aggregate, grad_pre)], axis=0).astype(BF)
    total_ref[...] = total
    grads = dot_t(adj, grad_agg)
    own_ref[...] = grads[:count]
    near, *far = peers
    halves = len(far) // 2
    blocks = [grads[z * count : (z + 1) * count] for z in range(1 + len(peers))]
    blocks = [blocks[near]] + [jnp.where(odd, blocks[a], blocks[b]) for a, b in zip(far[:halves], far[halves:])]
    for block, message in zip(blocks, messages):
        message[:count, :] = block.astype(BF)
        message[count:, :] = total


def rest_body(
    features_ref,
    local_ref,
    bound_ref,
    target_ref,
    w_self_ref,
    w_neigh_ref,
    rows_ref,
    pick_ref,
    near_ref,
    pre_ref,
    agg_ref,
    hidden_ref,
    out_ref,
):
    columns, width = rows_ref.shape
    features, near = features_ref[...], local_ref[...]
    chunk = math.gcd(columns, 512)
    ones = jnp.ones((max(chunk, near.shape[1]), width), BF)

    def move(c, totals):
        block = move_columns(bound_ref[...], target_ref[...], chunk, c)
        rows = rows_ref[pl.ds(pl.multiple_of(c * chunk, chunk), chunk), :]
        return totals[0] + dot(block, rows), totals[1] + dot(block, ones[:chunk])

    start = (dot(near, features), dot(near, ones[: near.shape[1]]))
    total, sums = lax.fori_loop(0, columns // chunk, move, start)
    aggregate = (total * (1.0 / (1.0 + sums))).astype(BF)
    preact = dot(features, w_self_ref[...]) + dot(aggregate, w_neigh_ref[...])
    hidden_ref[...] = (preact * jax.nn.sigmoid(preact)).astype(BF)
    odd = odd_core()
    half = pre_ref.shape[0] // 2
    grad_pre, grad_agg = pre_ref[...], agg_ref[...]
    grad_pre = jnp.where(odd, grad_pre[half:], grad_pre[:half])
    grad_agg = jnp.where(odd, grad_agg[half:], grad_agg[:half])
    spread = dot_t(pick_ref[...], grad_pre).astype(BF)
    out_ref[...] = dot_nt(spread, w_self_ref[...]) + dot_t(near_ref[...], grad_agg)


def column_body(peers, scale, total_ref, own_ref, *refs):
    refs, (out_ref, grads_ref) = refs[:-2], refs[-2:]
    rows = own_ref.shape[0]
    messages = by_peer(peers, None, refs)[1:]
    total = tree_sum([part.astype(F32) for part in [total_ref[...]] + [x[rows:] for x in messages]])
    out_ref[...] = (total * scale).astype(BF)
    grads = own_ref[...]
    for message in messages:
        grads = grads + message[:rows].astype(F32)
    grads_ref[...] = jnp.where(odd_core(), grads[rows // 2 :], grads[: rows // 2])


def features_body(hidden_ref, place_ref, local_grad_ref, grads_ref, hidden_out, out_ref):
    hidden_out[...] = hidden_ref[...]
    total = grads_ref[...]
    place = place_ref[...]
    high = total.astype(BF)
    low = (total - high.astype(F32)).astype(BF)
    out_ref[...] = (local_grad_ref[...] + dot(place, high) + dot(place, low)).astype(BF)


def order_body(peers, own_ref, *refs):
    refs, (self_ref, neigh_ref) = refs[:-2], refs[-2:]
    total = tree_sum([part.astype(F32) for part in by_peer(peers, own_ref[...], refs)])
    width = self_ref.shape[0]
    self_ref[...] = total[:width]
    neigh_ref[...] = total[width:]


def split_peers(size, near=1, swap=False):
    far = [k for k in range(size - 1, 0, -1) if k != near]
    if swap:
        return [near] + far[1::2] + far[::2]
    return [near] + far[::2] + far[1::2]


def local(
    features,
    adj_local,
    adj_bound,
    w_self,
    w_neigh,
    pub_rows,
    recv_pos,
    recv_count,
    target_mask,
    cotangent,
):
    dom_size, group_size = lax.axis_size("dom"), lax.axis_size("group")
    z_size = dom_size // 2
    row_count, width = features.shape
    pub_count = pub_rows.shape[1]
    wide = (row_count, width)
    devices = range(group_size * dom_size)

    def exchange(x, odd_step, even_step):
        return lax.ppermute(x, ("group", "dom"), [(a, a ^ (odd_step if a % 2 else even_step)) for a in devices])

    def over_core(x):
        return exchange(x, 1, 1)

    first = (
        pub_rows,
        features,
        target_mask.reshape(1, row_count),
        recv_pos,
        recv_count,
        adj_bound,
        cotangent,
        adj_local,
        w_self,
        w_neigh,
    )
    published, *first = pl.pallas_call(
        functools.partial(publish_body, len(first)),
        out_shape=[jax.ShapeDtypeStruct((pub_count, width), BF)]
        + [jax.ShapeDtypeStruct(x.shape, x.dtype) for x in first],
        in_specs=[HBM] * len(first),
        out_specs=[VMEM] * (1 + len(first)),
        scratch_shapes=[pltpu.SemaphoreType.DMA((len(first),))],
        compiler_params=PARAMS,
    )(*(in_hbm(x) for x in first))
    _, features, _, _, _, adj_bound, _, adj_local, w_self, w_neigh = first
    other = over_core(published)
    columns = dom_size * pub_count
    hits = row_count // BLOCK * HITS
    place, target, pick, near, pack = call(
        functools.partial(prepare_body, dom_size),
        [
            ((row_count, pub_count), BF),
            (recv_pos.shape, jnp.int32),
            ((hits, row_count), BF),
            ((hits, row_count), BF),
            ((hits, columns + 4 * width), F32),
        ],
        *first[:8],
    )
    other, pack = lax.optimization_barrier((other, pack))
    (pair,) = call(pair_body, [((2 * pub_count, width), BF)], published, other)
    def stage(near, far, peers, step, also=()):
        first, *rest = peers
        count = len(rest) // 2
        got = [exchange(near, step * first + 1, step * first + 1)]
        got += [exchange(x, step * a, step * b) for x, a, b in zip(far, rest[:count], rest[count:])]
        if also:
            got[-1], *also = lax.optimization_barrier((got[-1], *also))
        return got + [over_core(x) for x in got[1:]], also

    c_peers, z_peers, group_peers = split_peers(z_size, 1), split_peers(z_size, 3), split_peers(group_size, 2)
    got, _ = stage(pair, [pair] * (len(c_peers) // 2), c_peers, 2)
    square, both = (width, width), (2 * width, width)
    message = ((2 * pub_count + 2 * width, width), BF)
    (rows,) = call(functools.partial(rows_body, c_peers), [((columns, width), BF)], pair, *got)
    grad_pre, grad_agg, own_g, chip_w, *messages = call(
        functools.partial(target_body, z_peers),
        [((2 * hits, width), BF)] * 2 + [((2 * pub_count, width), F32), (both, BF)] + [message] * (1 + len(z_peers) // 2),
        w_self,
        w_neigh,
        pack,
        over_core(pack),
        rows,
    )
    hidden, local_grad = call(
        rest_body,
        [(wide, BF), (wide, F32)],
        features,
        adj_local,
        adj_bound,
        target,
        w_self,
        w_neigh,
        rows,
        pick,
        near,
        grad_pre,
        grad_agg,
    )
    got, (hidden, local_grad) = stage(messages[0], messages[1:], z_peers, 2, (hidden, local_grad))
    scale = 1.0 / math.sqrt(row_count * group_size * dom_size // 8)
    column_w, grads = call(
        functools.partial(column_body, z_peers, scale),
        [(both, BF), ((pub_count, width), F32)],
        chip_w,
        own_g,
        *got,
    )
    features_out = call(features_body, [(wide, BF)] * 2, hidden, place, local_grad, grads)
    got, (hidden, grad_features) = stage(
        column_w, [column_w] * (len(group_peers) // 2), group_peers, dom_size, features_out
    )
    grad_self, grad_neigh = call(
        functools.partial(order_body, group_peers), [(square, F32)] * 2, column_w, *got
    )
    return hidden, grad_features, grad_self, grad_neigh


def solution(mesh):
    rows = P(("group", "dom"), None)
    in_specs = (rows, rows, rows, P(), P(), rows, rows, rows, P(("group", "dom")), rows)
    return jax.shard_map(
        local, mesh=mesh, in_specs=in_specs, out_specs=(rows, rows, P(), P()), check_vma=False
    )
```

```python
import functools
import math

import jax
import jax.numpy as jnp
from jax import lax
from jax.experimental import pallas as pl
from jax.experimental.pallas import tpu as pltpu
from jax.sharding import PartitionSpec as P

BF = jnp.bfloat16
F32 = jnp.float32
BLOCK, HITS = 128, 16
VMEM = pl.BlockSpec(memory_space=pltpu.VMEM)
HBM = pl.BlockSpec(memory_space=pltpu.HBM)
PARAMS = pltpu.CompilerParams(vmem_limit_bytes=48 * 1024 * 1024)


def dot(a, b):
    return jnp.dot(a, b, preferred_element_type=F32)


def dot_t(a, b):
    return lax.dot_general(a, b, (((0,), (0,)), ((), ())), preferred_element_type=F32)


def dot_nt(a, b):
    return lax.dot_general(a, b, (((1,), (1,)), ((), ())), preferred_element_type=F32)


def one_hot(rows, targets):
    row = lax.broadcasted_iota(jnp.int32, (rows, targets.shape[1]), 0)
    return jnp.where(row == targets, 1.0, 0.0).astype(BF)


def in_hbm(x):
    return pltpu.with_memory_space_constraint(x, pltpu.HBM)


def call(body, outs, *args, flops=None):
    return pl.pallas_call(
        body,
        out_shape=[jax.ShapeDtypeStruct(shape, dtype) for shape, dtype in outs],
        in_specs=[VMEM] * len(args),
        out_specs=[VMEM] * len(outs),
        compiler_params=PARAMS,
        cost_estimate=flops and pl.CostEstimate(flops=flops, bytes_accessed=0, transcendentals=0),
    )(*args)


def odd_core():
    return lax.axis_index("dom") % 2 == 1


def tree_sum(parts):
    while len(parts) > 1:
        parts = [a + b for a, b in zip(parts[::2], parts[1::2])]
    return parts[0]


def load(pairs, sems):
    copies = [pltpu.make_async_copy(a, b, sems.at[i]) for i, (a, b) in enumerate(pairs)]
    for copy in copies:
        copy.start()
    return copies


def publish_body(count, *refs):
    sources, (out_ref, *targets), sems = refs[:count], refs[count:-1], refs[-1]
    pub, rows, *rest = load(list(zip(sources, targets)), sems)
    pub_ref, features_ref = targets[:2]
    pub_count = pub_ref.shape[1]
    square = (pub_count, pub_count)
    pub.wait()
    diagonal = lax.broadcasted_iota(jnp.int32, square, 0) == lax.broadcasted_iota(jnp.int32, square, 1)
    column = jnp.sum(jnp.where(diagonal, pub_ref[...].astype(F32), 0.0), axis=1, keepdims=True)
    row = lax.broadcasted_iota(jnp.int32, (pub_count, features_ref.shape[0]), 1)
    pick = jnp.where(row == column.astype(jnp.int32), 1.0, 0.0).astype(BF)
    rows.wait()
    out_ref[...] = dot(pick, features_ref[...]).astype(BF)
    for copy in rest:
        copy.wait()


def pair_body(own_ref, other_ref, out_ref):
    rows = own_ref.shape[0]
    odd = odd_core()
    own, other = own_ref[...], other_ref[...]
    out_ref[:rows, :] = jnp.where(odd, other, own)
    out_ref[rows:, :] = jnp.where(odd, own, other)


def move_columns(bound, target, chunk, c):
    return dot_nt(bound, one_hot(chunk, target - c * chunk)).astype(BF)


def prepare_body(
    dom_size,
    pub_ref,
    features_ref,
    mask_ref,
    pos_ref,
    count_ref,
    bound_ref,
    cot_ref,
    local_ref,
    place_ref,
    target_ref,
    pick_ref,
    near_ref,
    pack_ref,
):
    pub_count = pub_ref.shape[1]
    row_count, width = features_ref.shape
    place_ref[...] = one_hot(row_count, pub_ref[...])
    me = lax.axis_index("dom")
    chip = me - me % 2
    slots = pos_ref.shape[1]
    slot_rows = slots // dom_size
    lane = lax.broadcasted_iota(jnp.int32, (1, slots), 1)
    peer = lane // slot_rows
    limit = jnp.zeros((1, slots), jnp.int32)
    for j in range(dom_size):
        limit = jnp.where(peer == j, count_ref[0:1, j : j + 1], limit)
    in_use = lane % slot_rows < limit
    target = jnp.where(in_use, (peer ^ chip) * pub_count + pos_ref[...], -1)
    target_ref[...] = target
    blocks = row_count // BLOCK
    mask = jnp.concatenate(
        [
            jnp.broadcast_to(mask_ref[0:1, b * BLOCK : (b + 1) * BLOCK].astype(F32), (HITS, BLOCK))
            for b in range(blocks)
        ],
        axis=0,
    )
    before = lax.broadcasted_iota(jnp.int32, (BLOCK, BLOCK), 0) < lax.broadcasted_iota(jnp.int32, (BLOCK, BLOCK), 1)
    rank = dot(mask.astype(BF), jnp.where(before, 1.0, 0.0).astype(BF))
    row = lax.broadcasted_iota(jnp.int32, mask.shape, 0)
    hit = jnp.where(rank == (row % HITS).astype(F32), mask, 0.0)
    pick = jnp.concatenate([jnp.where(row // HITS == b, hit, 0.0) for b in range(blocks)], axis=1).astype(BF)
    pick_ref[...] = pick
    columns = dom_size * pub_count
    features = features_ref[...]
    near = dot(pick, local_ref[...]).astype(BF)
    near_ref[...] = near
    bound = dot(pick, bound_ref[...]).astype(BF)
    pack_ref[:, columns : columns + width] = dot(pick, features)
    pack_ref[:, columns + width : columns + 2 * width] = dot(pick, cot_ref[...])
    pack_ref[:, columns + 2 * width : columns + 3 * width] = dot(near, features)
    chunk = math.gcd(columns, 512)
    ones = jnp.ones((max(chunk, row_count), width), BF)

    def move(c, total):
        block = move_columns(bound, target, chunk, c)
        pack_ref[:, pl.ds(pl.multiple_of(c * chunk, chunk), chunk)] = block.astype(F32)
        return total + dot(block, ones[:chunk])

    sums = lax.fori_loop(0, columns // chunk, move, dot(near, ones[:row_count]))
    pack_ref[:, columns + 3 * width :] = 1.0 / (1.0 + sums)


def either(mine, others):
    odd = odd_core()
    pairs = [(a[...], b[...]) for a, b in zip(mine, others)]
    return [jnp.where(odd, a, b) for a, b in pairs] + [jnp.where(odd, b, a) for a, b in pairs]


def by_peer(peers, own, refs):
    near, *far = peers
    count = len(far) // 2
    parts = dict(zip(far, either(refs[1 : 1 + count], refs[1 + count : 1 + 2 * count])))
    parts |= {0: own, near: refs[0][...]}
    return [parts[k] for k in sorted(parts)]


def rows_body(peers, pair_ref, *refs):
    refs, out_ref = refs[:-1], refs[-1]
    count = pair_ref.shape[0]
    for z, pair in enumerate(by_peer(peers, pair_ref[...], refs)):
        out_ref[z * count : (z + 1) * count, :] = pair


def target_body(
    peers,
    w_self_ref,
    w_neigh_ref,
    pack_ref,
    got_pack_ref,
    rows_ref,
    pre_ref,
    agg_ref,
    own_ref,
    total_ref,
    *messages,
):
    count = rows_ref.shape[0] // (1 + len(peers))
    odd = odd_core()
    columns, width = rows_ref.shape
    own, other = pack_ref[...], got_pack_ref[...]
    pack = jnp.concatenate([jnp.where(odd, other, own), jnp.where(odd, own, other)], axis=0)
    adj = pack[:, :columns].astype(BF)
    features, cot, part, inv = (pack[:, columns + i * width : columns + (i + 1) * width] for i in range(4))
    features = features.astype(BF)
    aggregate = ((part + dot(adj, rows_ref[...])) * inv).astype(BF)
    preact = dot(features, w_self_ref[...]) + dot(aggregate, w_neigh_ref[...])
    sigma = jax.nn.sigmoid(preact)
    slope = sigma * (1.0 + preact * (1.0 - sigma))
    grad_pre = (cot * slope).astype(BF)
    grad_agg = (dot_nt(grad_pre, w_neigh_ref[...]) * inv).astype(BF)
    pre_ref[...] = grad_pre
    agg_ref[...] = grad_agg
    total = jnp.concatenate([dot_t(features, grad_pre), dot_t(aggregate, grad_pre)], axis=0).astype(BF)
    total_ref[...] = total
    grads = dot_t(adj, grad_agg)
    own_ref[...] = grads[:count]
    near, *far = peers
    halves = len(far) // 2
    blocks = [grads[z * count : (z + 1) * count] for z in range(1 + len(peers))]
    to_other = jnp.where(odd, blocks[near][: count // 2], blocks[near][count // 2 :])
    blocks = [to_other] + [jnp.where(odd, blocks[a], blocks[b]) for a, b in zip(far[:halves], far[halves:])]
    for block, message in zip(blocks, messages):
        message[: block.shape[0], :] = block.astype(BF)
        message[block.shape[0] :, :] = total


def rest_body(
    features_ref,
    local_ref,
    bound_ref,
    target_ref,
    w_self_ref,
    w_neigh_ref,
    rows_ref,
    pick_ref,
    near_ref,
    pre_ref,
    agg_ref,
    hidden_ref,
    out_ref,
):
    columns, width = rows_ref.shape
    features, near = features_ref[...], local_ref[...]
    chunk = math.gcd(columns, 512)
    ones = jnp.ones((max(chunk, near.shape[1]), width), BF)

    def move(c, totals):
        block = move_columns(bound_ref[...], target_ref[...], chunk, c)
        rows = rows_ref[pl.ds(pl.multiple_of(c * chunk, chunk), chunk), :]
        return totals[0] + dot(block, rows), totals[1] + dot(block, ones[:chunk])

    start = (dot(near, features), dot(near, ones[: near.shape[1]]))
    total, sums = lax.fori_loop(0, columns // chunk, move, start)
    aggregate = (total * (1.0 / (1.0 + sums))).astype(BF)
    preact = dot(features, w_self_ref[...]) + dot(aggregate, w_neigh_ref[...])
    hidden_ref[...] = (preact * jax.nn.sigmoid(preact)).astype(BF)
    odd = odd_core()
    half = pre_ref.shape[0] // 2
    grad_pre, grad_agg = pre_ref[...], agg_ref[...]
    grad_pre = jnp.where(odd, grad_pre[half:], grad_pre[:half])
    grad_agg = jnp.where(odd, grad_agg[half:], grad_agg[:half])
    spread = dot_t(pick_ref[...], grad_pre).astype(BF)
    out_ref[...] = dot_nt(spread, w_self_ref[...]) + dot_t(near_ref[...], grad_agg)


def near_body(total_ref, own_ref, got_ref, sum_ref, grads_ref):
    rows = own_ref.shape[0] // 2
    odd = odd_core()
    sum_ref[...] = total_ref[...].astype(F32) + got_ref[rows:, :].astype(F32)
    own = jnp.where(odd, own_ref[rows:, :], own_ref[:rows, :])
    grads_ref[...] = own + got_ref[:rows, :].astype(F32)


def span(size, first):
    out = [0]
    for k in [first, *range(1, size)]:
        if k not in out:
            out += [j ^ k for j in out]
    return out


def column_body(peers, scale, sum_ref, near_ref, *refs):
    refs, (out_ref, grads_ref) = refs[:-2], refs[-2:]
    rows = near_ref.shape[0]
    near, *far = peers
    messages = dict(zip(far, either(refs[: len(far) // 2], refs[len(far) // 2 :])))
    messages = [messages[k] for k in span(1 + len(peers), near)[2:]]
    parts = [message[2 * rows :].astype(F32) for message in messages]
    total = tree_sum([sum_ref[...]] + [x + y for x, y in zip(parts[::2], parts[1::2])])
    out_ref[...] = (total * scale).astype(BF)
    grads = near_ref[...]
    for message in messages:
        grads = grads + jnp.where(odd_core(), message[rows : 2 * rows], message[:rows]).astype(F32)
    grads_ref[...] = grads


def features_body(hidden_ref, place_ref, local_grad_ref, grads_ref, hidden_out, out_ref):
    hidden_out[...] = hidden_ref[...]
    total = grads_ref[...]
    place = place_ref[...]
    high = total.astype(BF)
    low = (total - high.astype(F32)).astype(BF)
    out_ref[...] = (local_grad_ref[...] + dot(place, high) + dot(place, low)).astype(BF)


def order_body(peers, own_ref, *refs):
    refs, (self_ref, neigh_ref) = refs[:-2], refs[-2:]
    total = tree_sum([part.astype(F32) for part in by_peer(peers, own_ref[...], refs)])
    width = self_ref.shape[0]
    self_ref[...] = total[:width]
    neigh_ref[...] = total[width:]


def split_peers(size, near=1, swap=False):
    far = [k for k in range(size - 1, 0, -1) if k != near]
    if swap:
        return [near] + far[1::2] + far[::2]
    return [near] + far[::2] + far[1::2]


def local(
    features,
    adj_local,
    adj_bound,
    w_self,
    w_neigh,
    pub_rows,
    recv_pos,
    recv_count,
    target_mask,
    cotangent,
):
    dom_size, group_size = lax.axis_size("dom"), lax.axis_size("group")
    z_size = dom_size // 2
    row_count, width = features.shape
    pub_count = pub_rows.shape[1]
    wide = (row_count, width)
    devices = range(group_size * dom_size)

    def exchange(x, odd_step, even_step):
        return lax.ppermute(x, ("group", "dom"), [(a, a ^ (odd_step if a % 2 else even_step)) for a in devices])

    def over_core(x):
        return exchange(x, 1, 1)

    first = (
        pub_rows,
        features,
        target_mask.reshape(1, row_count),
        recv_pos,
        recv_count,
        adj_bound,
        cotangent,
        adj_local,
        w_self,
        w_neigh,
    )
    published, *first = pl.pallas_call(
        functools.partial(publish_body, len(first)),
        out_shape=[jax.ShapeDtypeStruct((pub_count, width), BF)]
        + [jax.ShapeDtypeStruct(x.shape, x.dtype) for x in first],
        in_specs=[HBM] * len(first),
        out_specs=[VMEM] * (1 + len(first)),
        scratch_shapes=[pltpu.SemaphoreType.DMA((len(first),))],
        compiler_params=PARAMS,
    )(*(in_hbm(x) for x in first))
    _, features, _, _, _, adj_bound, _, adj_local, w_self, w_neigh = first
    other = over_core(published)
    columns = dom_size * pub_count
    hits = row_count // BLOCK * HITS
    place, target, pick, near, pack = call(
        functools.partial(prepare_body, dom_size),
        [
            ((row_count, pub_count), BF),
            (recv_pos.shape, jnp.int32),
            ((hits, row_count), BF),
            ((hits, row_count), BF),
            ((hits, columns + 4 * width), F32),
        ],
        *first[:8],
    )
    other, pack = lax.optimization_barrier((other, pack))
    (pair,) = call(pair_body, [((2 * pub_count, width), BF)], published, other)
    def stage(near, far, peers, step, also=()):
        first, *rest = peers
        count = len(rest) // 2
        got = [exchange(near, step * first + 1, step * first + 1)]
        got += [exchange(x, step * a, step * b) for x, a, b in zip(far, rest[:count], rest[count:])]
        if also:
            got[-1], *also = lax.optimization_barrier((got[-1], *also))
        return got + [over_core(x) for x in got[1:]], also

    c_peers, z_peers, group_peers = split_peers(z_size, 1), split_peers(z_size, 3), split_peers(group_size, 2)
    got, _ = stage(pair, [pair] * (len(c_peers) // 2), c_peers, 2)
    square, both = (width, width), (2 * width, width)
    message = ((2 * pub_count + 2 * width, width), BF)
    (rows,) = call(functools.partial(rows_body, c_peers), [((columns, width), BF)], pair, *got)
    grad_pre, grad_agg, own_g, chip_w, *messages = call(
        functools.partial(target_body, z_peers),
        [((2 * hits, width), BF)] * 2 + [((2 * pub_count, width), F32), (both, BF)] + [((pub_count + 2 * width, width), BF)] + [message] * (len(z_peers) // 2),
        w_self,
        w_neigh,
        pack,
        over_core(pack),
        rows,
    )
    hidden, local_grad = call(
        rest_body,
        [(wide, BF), (wide, F32)],
        features,
        adj_local,
        adj_bound,
        target,
        w_self,
        w_neigh,
        rows,
        pick,
        near,
        grad_pre,
        grad_agg,
    )
    got, (hidden, local_grad) = stage(messages[0], messages[1:], z_peers, 2, (hidden, local_grad))
    scale = 1.0 / math.sqrt(row_count * group_size * dom_size // 8)
    near_w, near_g = call(
        near_body, [(both, F32), ((pub_count, width), F32)], chip_w, own_g, got[0], flops=2 * 10**9
    )
    column_w, grads = call(
        functools.partial(column_body, z_peers, scale),
        [(both, BF), ((pub_count, width), F32)],
        near_w,
        near_g,
        *got[1:],
    )
    features_out = call(features_body, [(wide, BF)] * 2, hidden, place, local_grad, grads)
    got, (hidden, grad_features) = stage(
        column_w, [column_w] * (len(group_peers) // 2), group_peers, dom_size, features_out
    )
    grad_self, grad_neigh = call(
        functools.partial(order_body, group_peers), [(square, F32)] * 2, column_w, *got
    )
    return hidden, grad_features, grad_self, grad_neigh


def solution(mesh):
    rows = P(("group", "dom"), None)
    in_specs = (rows, rows, rows, P(), P(), rows, rows, rows, P(("group", "dom")), rows)
    return jax.shard_map(
        local, mesh=mesh, in_specs=in_specs, out_specs=(rows, rows, P(), P()), check_vma=False
    )
```

```python
import functools
import math

import jax
import jax.numpy as jnp
from jax import lax
from jax.experimental import pallas as pl
from jax.experimental.pallas import tpu as pltpu
from jax.sharding import PartitionSpec as P

BF = jnp.bfloat16
F32 = jnp.float32
BLOCK, HITS = 128, 16
VMEM = pl.BlockSpec(memory_space=pltpu.VMEM)
HBM = pl.BlockSpec(memory_space=pltpu.HBM)
PARAMS = pltpu.CompilerParams(vmem_limit_bytes=48 * 1024 * 1024)


def dot(a, b):
    return jnp.dot(a, b, preferred_element_type=F32)


def dot_t(a, b):
    return lax.dot_general(a, b, (((0,), (0,)), ((), ())), preferred_element_type=F32)


def dot_nt(a, b):
    return lax.dot_general(a, b, (((1,), (1,)), ((), ())), preferred_element_type=F32)


def one_hot(rows, targets):
    row = lax.broadcasted_iota(jnp.int32, (rows, targets.shape[1]), 0)
    return jnp.where(row == targets, 1.0, 0.0).astype(BF)


def in_hbm(x):
    return pltpu.with_memory_space_constraint(x, pltpu.HBM)


def call(body, outs, *args, flops=None):
    return pl.pallas_call(
        body,
        out_shape=[jax.ShapeDtypeStruct(shape, dtype) for shape, dtype in outs],
        in_specs=[VMEM] * len(args),
        out_specs=[VMEM] * len(outs),
        compiler_params=PARAMS,
        cost_estimate=flops and pl.CostEstimate(flops=flops, bytes_accessed=0, transcendentals=0),
    )(*args)


def odd_core():
    return lax.axis_index("dom") % 2 == 1


def tree_sum(parts):
    while len(parts) > 1:
        parts = [a + b for a, b in zip(parts[::2], parts[1::2])]
    return parts[0]


def load(pairs, sems):
    copies = [pltpu.make_async_copy(a, b, sems.at[i]) for i, (a, b) in enumerate(pairs)]
    for copy in copies:
        copy.start()
    return copies


def publish_body(count, *refs):
    sources, (out_ref, *targets), sems = refs[:count], refs[count:-1], refs[-1]
    pub, rows, *rest = load(list(zip(sources, targets)), sems)
    pub_ref, features_ref = targets[:2]
    pub_count = pub_ref.shape[1]
    square = (pub_count, pub_count)
    pub.wait()
    diagonal = lax.broadcasted_iota(jnp.int32, square, 0) == lax.broadcasted_iota(jnp.int32, square, 1)
    column = jnp.sum(jnp.where(diagonal, pub_ref[...].astype(F32), 0.0), axis=1, keepdims=True)
    row = lax.broadcasted_iota(jnp.int32, (pub_count, features_ref.shape[0]), 1)
    pick = jnp.where(row == column.astype(jnp.int32), 1.0, 0.0).astype(BF)
    rows.wait()
    out_ref[...] = dot(pick, features_ref[...]).astype(BF)
    for copy in rest:
        copy.wait()


def pair_body(own_ref, other_ref, out_ref):
    rows = own_ref.shape[0]
    odd = odd_core()
    own, other = own_ref[...], other_ref[...]
    out_ref[:rows, :] = jnp.where(odd, other, own)
    out_ref[rows:, :] = jnp.where(odd, own, other)


def move_columns(bound, target, chunk, c):
    return dot_nt(bound, one_hot(chunk, target - c * chunk)).astype(BF)


def prepare_body(
    dom_size,
    pub_ref,
    features_ref,
    mask_ref,
    pos_ref,
    count_ref,
    bound_ref,
    cot_ref,
    local_ref,
    place_ref,
    target_ref,
    pick_ref,
    near_ref,
    pack_ref,
):
    pub_count = pub_ref.shape[1]
    row_count, width = features_ref.shape
    place_ref[...] = one_hot(row_count, pub_ref[...])
    me = lax.axis_index("dom")
    chip = me - me % 2
    slots = pos_ref.shape[1]
    slot_rows = slots // dom_size
    lane = lax.broadcasted_iota(jnp.int32, (1, slots), 1)
    peer = lane // slot_rows
    limit = jnp.zeros((1, slots), jnp.int32)
    for j in range(dom_size):
        limit = jnp.where(peer == j, count_ref[0:1, j : j + 1], limit)
    in_use = lane % slot_rows < limit
    target = jnp.where(in_use, (peer ^ chip) * pub_count + pos_ref[...], -1)
    target_ref[...] = target
    blocks = row_count // BLOCK
    mask = jnp.concatenate(
        [
            jnp.broadcast_to(mask_ref[0:1, b * BLOCK : (b + 1) * BLOCK].astype(F32), (HITS, BLOCK))
            for b in range(blocks)
        ],
        axis=0,
    )
    before = lax.broadcasted_iota(jnp.int32, (BLOCK, BLOCK), 0) < lax.broadcasted_iota(jnp.int32, (BLOCK, BLOCK), 1)
    rank = dot(mask.astype(BF), jnp.where(before, 1.0, 0.0).astype(BF))
    row = lax.broadcasted_iota(jnp.int32, mask.shape, 0)
    hit = jnp.where(rank == (row % HITS).astype(F32), mask, 0.0)
    pick = jnp.concatenate([jnp.where(row // HITS == b, hit, 0.0) for b in range(blocks)], axis=1).astype(BF)
    pick_ref[...] = pick
    columns = dom_size * pub_count
    features = features_ref[...]
    near = dot(pick, local_ref[...]).astype(BF)
    near_ref[...] = near
    bound = dot(pick, bound_ref[...]).astype(BF)
    pack_ref[:, columns : columns + width] = dot(pick, features)
    pack_ref[:, columns + width : columns + 2 * width] = dot(pick, cot_ref[...])
    pack_ref[:, columns + 2 * width : columns + 3 * width] = dot(near, features)
    chunk = math.gcd(columns, 512)
    ones = jnp.ones((max(chunk, row_count), width), BF)

    def move(c, total):
        block = move_columns(bound, target, chunk, c)
        pack_ref[:, pl.ds(pl.multiple_of(c * chunk, chunk), chunk)] = block.astype(F32)
        return total + dot(block, ones[:chunk])

    sums = lax.fori_loop(0, columns // chunk, move, dot(near, ones[:row_count]))
    pack_ref[:, columns + 3 * width :] = 1.0 / (1.0 + sums)


def either(mine, others):
    odd = odd_core()
    pairs = [(a[...], b[...]) for a, b in zip(mine, others)]
    return [jnp.where(odd, a, b) for a, b in pairs] + [jnp.where(odd, b, a) for a, b in pairs]


def by_peer(peers, own, refs):
    near, *far = peers
    count = len(far) // 2
    parts = dict(zip(far, either(refs[1 : 1 + count], refs[1 + count : 1 + 2 * count])))
    parts |= {0: own, near: refs[0][...]}
    return [parts[k] for k in sorted(parts)]


def rows_body(peers, pair_ref, *refs):
    refs, out_ref = refs[:-1], refs[-1]
    count = pair_ref.shape[0]
    for z, pair in enumerate(by_peer(peers, pair_ref[...], refs)):
        out_ref[z * count : (z + 1) * count, :] = pair


def target_body(
    peers,
    w_self_ref,
    w_neigh_ref,
    pack_ref,
    got_pack_ref,
    rows_ref,
    pre_ref,
    agg_ref,
    own_ref,
    total_ref,
    *messages,
):
    count = rows_ref.shape[0] // (1 + len(peers))
    odd = odd_core()
    columns, width = rows_ref.shape
    own, other = pack_ref[...], got_pack_ref[...]
    pack = jnp.concatenate([jnp.where(odd, other, own), jnp.where(odd, own, other)], axis=0)
    adj = pack[:, :columns].astype(BF)
    features, cot, part, inv = (pack[:, columns + i * width : columns + (i + 1) * width] for i in range(4))
    features = features.astype(BF)
    aggregate = ((part + dot(adj, rows_ref[...])) * inv).astype(BF)
    preact = dot(features, w_self_ref[...]) + dot(aggregate, w_neigh_ref[...])
    sigma = jax.nn.sigmoid(preact)
    slope = sigma * (1.0 + preact * (1.0 - sigma))
    grad_pre = (cot * slope).astype(BF)
    grad_agg = (dot_nt(grad_pre, w_neigh_ref[...]) * inv).astype(BF)
    pre_ref[...] = grad_pre
    agg_ref[...] = grad_agg
    total = jnp.concatenate([dot_t(features, grad_pre), dot_t(aggregate, grad_pre)], axis=0).astype(BF)
    total_ref[...] = total
    grads = dot_t(adj, grad_agg)
    own_ref[...] = grads[:count]
    near, *far = peers
    halves = len(far) // 2
    blocks = [grads[z * count : (z + 1) * count] for z in range(1 + len(peers))]
    to_other = jnp.where(odd, blocks[near][: count // 2], blocks[near][count // 2 :])
    blocks = [to_other] + [jnp.where(odd, blocks[a], blocks[b]) for a, b in zip(far[:halves], far[halves:])]
    for block, message in zip(blocks, messages):
        message[: block.shape[0], :] = block.astype(BF)
        message[block.shape[0] :, :] = total


def rest_body(
    features_ref,
    local_ref,
    bound_ref,
    target_ref,
    w_self_ref,
    w_neigh_ref,
    rows_ref,
    pick_ref,
    near_ref,
    pre_ref,
    agg_ref,
    hidden_ref,
    out_ref,
):
    columns, width = rows_ref.shape
    features, near = features_ref[...], local_ref[...]
    chunk = math.gcd(columns, 512)
    ones = jnp.ones((max(chunk, near.shape[1]), width), BF)

    def move(c, totals):
        block = move_columns(bound_ref[...], target_ref[...], chunk, c)
        rows = rows_ref[pl.ds(pl.multiple_of(c * chunk, chunk), chunk), :]
        return totals[0] + dot(block, rows), totals[1] + dot(block, ones[:chunk])

    start = (dot(near, features), dot(near, ones[: near.shape[1]]))
    total, sums = lax.fori_loop(0, columns // chunk, move, start)
    aggregate = (total * (1.0 / (1.0 + sums))).astype(BF)
    preact = dot(features, w_self_ref[...]) + dot(aggregate, w_neigh_ref[...])
    hidden_ref[...] = (preact * jax.nn.sigmoid(preact)).astype(BF)
    odd = odd_core()
    half = pre_ref.shape[0] // 2
    grad_pre, grad_agg = pre_ref[...], agg_ref[...]
    grad_pre = jnp.where(odd, grad_pre[half:], grad_pre[:half])
    grad_agg = jnp.where(odd, grad_agg[half:], grad_agg[:half])
    spread = dot_t(pick_ref[...], grad_pre).astype(BF)
    out_ref[...] = dot_nt(spread, w_self_ref[...]) + dot_t(near_ref[...], grad_agg)


def near_body(total_ref, own_ref, got_ref, sum_ref, grads_ref):
    rows = own_ref.shape[0] // 2
    odd = odd_core()
    sum_ref[...] = total_ref[...].astype(F32) + got_ref[rows:, :].astype(F32)
    own = jnp.where(odd, own_ref[rows:, :], own_ref[:rows, :])
    grads_ref[...] = own + got_ref[:rows, :].astype(F32)


def span(size, first):
    out = [0]
    for k in [first, *range(1, size)]:
        if k not in out:
            out += [j ^ k for j in out]
    return out


def column_body(peers, scale, sum_ref, near_ref, *refs):
    refs, (out_ref, grads_ref) = refs[:-2], refs[-2:]
    rows = near_ref.shape[0]
    near, *far = peers
    messages = dict(zip(far, either(refs[: len(far) // 2], refs[len(far) // 2 :])))
    messages = [messages[k] for k in span(1 + len(peers), near)[2:]]
    parts = [message[2 * rows :].astype(F32) for message in messages]
    total = tree_sum([sum_ref[...]] + [x + y for x, y in zip(parts[::2], parts[1::2])])
    out_ref[...] = (total * scale).astype(BF)
    grads = near_ref[...]
    for message in messages:
        grads = grads + jnp.where(odd_core(), message[rows : 2 * rows], message[:rows]).astype(F32)
    grads_ref[...] = grads


def features_body(hidden_ref, place_ref, local_grad_ref, grads_ref, hidden_out, out_ref):
    hidden_out[...] = hidden_ref[...]
    total = grads_ref[...]
    place = place_ref[...]
    high = total.astype(BF)
    low = (total - high.astype(F32)).astype(BF)
    out_ref[...] = (local_grad_ref[...] + dot(place, high) + dot(place, low)).astype(BF)


def order_body(peers, own_ref, *refs):
    refs, (self_ref, neigh_ref) = refs[:-2], refs[-2:]
    total = tree_sum([part.astype(F32) for part in by_peer(peers, own_ref[...], refs)])
    width = self_ref.shape[0]
    self_ref[...] = total[:width]
    neigh_ref[...] = total[width:]


def split_peers(size, near=1, swap=False):
    far = [k for k in range(size - 1, 0, -1) if k != near]
    if swap:
        return [near] + far[1::2] + far[::2]
    return [near] + far[::2] + far[1::2]


def local(
    features,
    adj_local,
    adj_bound,
    w_self,
    w_neigh,
    pub_rows,
    recv_pos,
    recv_count,
    target_mask,
    cotangent,
):
    dom_size, group_size = lax.axis_size("dom"), lax.axis_size("group")
    z_size = dom_size // 2
    row_count, width = features.shape
    pub_count = pub_rows.shape[1]
    wide = (row_count, width)
    devices = range(group_size * dom_size)

    def exchange(x, odd_step, even_step):
        return lax.ppermute(x, ("group", "dom"), [(a, a ^ (odd_step if a % 2 else even_step)) for a in devices])

    def over_core(x):
        return exchange(x, 1, 1)

    first = (
        pub_rows,
        features,
        target_mask.reshape(1, row_count),
        recv_pos,
        recv_count,
        adj_bound,
        cotangent,
        adj_local,
        w_self,
        w_neigh,
    )
    published, *first = pl.pallas_call(
        functools.partial(publish_body, len(first)),
        out_shape=[jax.ShapeDtypeStruct((pub_count, width), BF)]
        + [jax.ShapeDtypeStruct(x.shape, x.dtype) for x in first],
        in_specs=[HBM] * len(first),
        out_specs=[VMEM] * (1 + len(first)),
        scratch_shapes=[pltpu.SemaphoreType.DMA((len(first),))],
        compiler_params=PARAMS,
    )(*(in_hbm(x) for x in first))
    _, features, _, _, _, adj_bound, _, adj_local, w_self, w_neigh = first
    other = over_core(published)
    columns = dom_size * pub_count
    hits = row_count // BLOCK * HITS
    place, target, pick, near, pack = call(
        functools.partial(prepare_body, dom_size),
        [
            ((row_count, pub_count), BF),
            (recv_pos.shape, jnp.int32),
            ((hits, row_count), BF),
            ((hits, row_count), BF),
            ((hits, columns + 4 * width), F32),
        ],
        *first[:8],
    )
    other, pack = lax.optimization_barrier((other, pack))
    (pair,) = call(pair_body, [((2 * pub_count, width), BF)], published, other)
    def stage(near, far, peers, step, also=()):
        first, *rest = peers
        count = len(rest) // 2
        got = [exchange(near, step * first + 1, step * first + 1)]
        got += [exchange(x, step * a, step * b) for x, a, b in zip(far, rest[:count], rest[count:])]
        if also:
            got[-1], *also = lax.optimization_barrier((got[-1], *also))
        return got + [over_core(x) for x in got[1:]], also

    c_peers, z_peers, group_peers = split_peers(z_size, 1), split_peers(z_size, 3), split_peers(group_size, 2)
    got, _ = stage(pair, [pair] * (len(c_peers) // 2), c_peers, 2)
    square, both = (width, width), (2 * width, width)
    message = ((2 * pub_count + 2 * width, width), BF)
    (rows,) = call(functools.partial(rows_body, c_peers), [((columns, width), BF)], pair, *got)
    grad_pre, grad_agg, own_g, chip_w, *messages = call(
        functools.partial(target_body, z_peers),
        [((2 * hits, width), BF)] * 2 + [((2 * pub_count, width), F32), (both, BF)] + [((pub_count + 2 * width, width), BF)] + [message] * (len(z_peers) // 2),
        w_self,
        w_neigh,
        pack,
        over_core(pack),
        rows,
    )
    hidden, local_grad = call(
        rest_body,
        [(wide, BF), (wide, F32)],
        features,
        adj_local,
        adj_bound,
        target,
        w_self,
        w_neigh,
        rows,
        pick,
        near,
        grad_pre,
        grad_agg,
    )
    got, (hidden, local_grad) = stage(messages[0], messages[1:], z_peers, 2, (hidden, local_grad))
    scale = 1.0 / math.sqrt(row_count * group_size * dom_size // 8)
    near_w, near_g = call(
        near_body, [(both, F32), ((pub_count, width), F32)], chip_w, own_g, got[0], flops=2 * 10**9
    )
    column_w, grads = call(
        functools.partial(column_body, z_peers, scale),
        [(both, BF), ((pub_count, width), F32)],
        near_w,
        near_g,
        *got[1:],
    )
    hidden, grad_features = call(features_body, [(wide, BF)] * 2, hidden, place, local_grad, grads)
    got, _ = stage(column_w, [column_w] * (len(group_peers) // 2), group_peers, dom_size)
    grad_self, grad_neigh = call(
        functools.partial(order_body, group_peers), [(square, F32)] * 2, column_w, *got
    )
    return hidden, grad_features, grad_self, grad_neigh


def solution(mesh):
    rows = P(("group", "dom"), None)
    in_specs = (rows, rows, rows, P(), P(), rows, rows, rows, P(("group", "dom")), rows)
    return jax.shard_map(
        local, mesh=mesh, in_specs=in_specs, out_specs=(rows, rows, P(), P()), check_vma=False
    )
```
